256 devices in a mesh: seg: 32 (over z_lo, x, y), gx: 8 (over z_hi, core).
Axes of the slice: x: 4, y: 4, z: 8 (z_hi: 4, z_lo: 2; z = z_hi * 2 + z_lo), core: 2. Of those that a mesh axis runs over, the one named last changes fastest.
Arguments:
- krylov: float32 [32, 8, 256, 1024], P('seg', None, 'gx')
- advect_x: float32 [32, 256, 1024], P('seg', 'gx'), may hold values from -0.18 to 0.18
- advect_y: float32 [32, 256, 1024], P('seg', 'gx'), may hold values from -0.18 to 0.18
- step_counts: int32 [32], P('seg'), may hold values from 1 to 4, as said below
- drifts: int32 [32], P('seg'), may hold values from 0 to 16, as said below
Outputs:
- product: float32 [32, 8, 256, 1024], P('seg', None, 'gx')
- gram: float32 [8, 8], replicated
The draws below stay inside these ranges and needn't reach their ends.
Inputs may be any that keep to these rules, and one draw needn't show every extreme that they name: `step_counts`: some segment takes exactly 4 steps. Some segment drifts by exactly 16 cells.
All inputs are finite; a program needn't handle non-finite values.
Results may differ from the reference program's by a relative error of at most 0.0003.
Values sent between devices are 32-bit elements; how exact they have to be, the bound alone decides.
No kernel may reach another device: no remote copies, remote signals or barrier semaphores. Data moves between devices by JAX's collectives and lax.ppermute only.
A program may use at most 64 MiB of HBM per device.

```python
import math
import jax
import jax.numpy as jnp
from jax import lax

BLOCK = 8
NY = 1024
STEPS = 4
DRIFT = 16
SEGS = 32
NX = 256


def draw_krylov(key, part):
    key = jax.random.fold_in(key, 11)
    first = jax.random.fold_in(key, 0)
    second = jax.random.fold_in(key, 1)
    fourth = jax.random.fold_in(key, 3)
    fifth = jax.random.fold_in(key, 4)
    shape = (SEGS, BLOCK, NX, NY)
    seg_scale = 1.0 + 2.0 * jnp.arange(SEGS, dtype=jnp.float32) / max(SEGS - 1, 1)
    column = jnp.exp(jax.random.uniform(second, (BLOCK, 1, NY), jnp.float32) * math.log(10.0)) / 4.64
    amount = jax.random.uniform(fourth, (SEGS, BLOCK, 1, 1), jnp.float32, 0.5, 1.5)
    phase = jax.random.uniform(fifth, (BLOCK, 1, 1), jnp.float32, -math.pi, math.pi)
    xpos = jnp.arange(NX, dtype=jnp.float32)[None, :, None]
    ypos = jnp.arange(NY, dtype=jnp.float32)[None, None, :]
    wave = jnp.cos(2.0 * math.pi * xpos / NX + phase) * jnp.sin(math.pi * (ypos + 0.5) / NY)
    smooth = 1.6 * amount * wave[None]
    field = jax.random.normal(first, shape, jnp.float32) * column + smooth
    return (field * seg_scale[:, None, None, None]).astype(jnp.float32)


def draw_step_counts(key, part):
    key = jax.random.fold_in(key, 23)
    first, second = jax.random.split(key)
    counts = jax.random.randint(first, (SEGS,), 1, STEPS + 1)
    where_full = jax.random.randint(second, (), 0, SEGS)
    return counts.at[where_full].set(STEPS).astype(jnp.int32)


def draw_drifts(key, part):
    key = jax.random.fold_in(key, 37)
    first, second = jax.random.split(key)
    values = jax.random.randint(first, (SEGS,), 0, DRIFT + 1)
    where_full = jax.random.randint(second, (), 0, SEGS)
    return values.at[where_full].set(DRIFT).astype(jnp.int32)


def level_of(stream_key, extent, cuts, smallest, high):
    gain, own = 1.0, jax.random.fold_in(stream_key, 6)
    for position, shards_of in cuts:
        draws = jnp.exp(jax.random.uniform(jax.random.fold_in(own, position), (shards_of,), jnp.float32, smallest / len(cuts), high / len(cuts)))
        gain = gain * jnp.repeat(draws, extent[position] // shards_of).reshape([-1 if axis == position else 1 for axis in range(len(extent))])
    return gain


def setup_inputs(seed: int = 0) -> dict:
    streams_of = jax.random.split(jax.random.key(seed), 6)
    krylov = draw_krylov(jax.random.fold_in(streams_of[5], 71), 0)
    advect_x = jnp.clip(jax.random.uniform(streams_of[1], (SEGS, NX, NY), jnp.float32, -0.18, 0.18) * level_of(streams_of[1], (SEGS, NX, NY), ((0, 32), (1, 8)), -0.4, 0.0), -0.18, 0.18)
    advect_y = jnp.clip(jax.random.uniform(streams_of[2], (SEGS, NX, NY), jnp.float32, -0.18, 0.18) * level_of(streams_of[2], (SEGS, NX, NY), ((0, 32), (1, 8)), -0.4, 0.0), -0.18, 0.18)
    step_counts = draw_step_counts(jax.random.fold_in(streams_of[5], 71), 0)
    drifts = draw_drifts(jax.random.fold_in(streams_of[5], 71), 0)
    return {"krylov": krylov, "advect_x": advect_x, "advect_y": advect_y, "step_counts": step_counts, "drifts": drifts}


def tangent_step(field, coef_x, coef_y):
    east = jnp.roll(field, -1, axis=1)
    west = jnp.roll(field, 1, axis=1)
    zeros = jnp.zeros_like(field[:, :, :1])
    north = jnp.concatenate([field[:, :, 1:], zeros], axis=2)
    south = jnp.concatenate([zeros, field[:, :, :-1]], axis=2)
    return field + 0.2 * (east + west + north + south - 4.0 * field) - coef_x * (east - west) - coef_y * (north - south)


def one_segment(items):
    start, coef_x, coef_y, count, shift_by = items
    field = start
    for section in range(STEPS):
        stepped = tangent_step(field, coef_x[None], coef_y[None])
        field = jnp.where(section < count, stepped, field)
    return jnp.roll(field, shift_by, axis=1)


def pair_sum(items):
    left, right = items
    return jnp.einsum("bxy,cxy->bc", left, right, precision=lax.Precision.HIGHEST)


def reference(krylov, advect_x, advect_y, step_counts, drifts):
    moved = lax.map(one_segment, (krylov, advect_x, advect_y, step_counts, drifts))
    earlier = jnp.concatenate([moved[-1:], moved[:-1]], axis=0)
    product = krylov - earlier
    total = jnp.sum(lax.map(pair_sum, (krylov, product)), axis=0)
    gram = total / jnp.float32(SEGS * NX * NY)
    return product, gram
```

```python
import functools
import jax
import jax.numpy as jnp
from jax import lax
from jax.experimental import pallas as pl
from jax.experimental.pallas import tpu as pltpu
from jax.sharding import PartitionSpec as P

STEPS = 4
DRIFT = 16
TILE = 8

VMEM = pl.BlockSpec(memory_space=pltpu.VMEM)
SMEM = pl.BlockSpec(memory_space=pltpu.SMEM)
LIMIT = 32 * 1024 * 1024


def shift_pairs(count, by):
    return [(i, (i + by) % count) for i in range(count)]


def weights(ax, ay):
    col = lax.broadcasted_iota(jnp.int32, ax.shape, 1)
    last = ax.shape[1] - 1
    return (
        0.2 - ax,
        0.2 + ax,
        jnp.where(col == last, 0.0, 0.2 - ay),
        jnp.where(col == 0, 0.0, 0.2 + ay),
    )


def step(q, we, ww, wn, ws):
    rows, cols = q.shape
    return (
        0.2 * q
        + we * pltpu.roll(q, rows - 1, 0)
        + ww * pltpu.roll(q, 1, 0)
        + wn * pltpu.roll(q, cols - 1, 1)
        + ws * pltpu.roll(q, 1, 1)
    )


def inner_kernel(count_ref, k_ref, ax_ref, ay_ref, mid_ref, low_ref, high_ref, q_ref, w_ref):
    vectors, rows, _ = k_ref.shape
    for i, w in enumerate(weights(ax_ref[...], ay_ref[...])):
        w_ref[i] = w
    q_ref[...] = k_ref[...]

    @pl.loop(0, count_ref[0])
    def _(_):
        for b in range(vectors):
            q_ref[b] = step(q_ref[b], w_ref[0], w_ref[1], w_ref[2], w_ref[3])

    mid_ref[...] = q_ref[:, TILE : rows - TILE]
    low_ref[...] = q_ref[:, :TILE]
    high_ref[...] = q_ref[:, rows - TILE :]


def outer_kernel(
    count_ref, k_ref, ax_ref, ay_ref, left_ref, right_ref, low_ref, high_ref, lo_ref, hi_ref, q_ref, w_ref
):
    vectors, rows, _ = k_ref.shape

    def around(strip, at):
        return jnp.concatenate(
            [strip[rows - TILE :], right_ref[at], left_ref[at], strip[:TILE]], axis=0
        )

    for i, w in enumerate(weights(around(ax_ref, vectors), around(ay_ref, vectors + 1))):
        w_ref[i] = w
    for b in range(vectors):
        q_ref[b] = around(k_ref.at[b], b)

    @pl.loop(0, count_ref[0])
    def _(_):
        for b in range(vectors):
            q_ref[b] = step(q_ref[b], w_ref[0], w_ref[1], w_ref[2], w_ref[3])

    row = lax.broadcasted_iota(jnp.int32, lo_ref.shape[1:], 0)
    for b in range(vectors):
        hi_ref[b] = jnp.where(row < TILE - STEPS, high_ref[b], q_ref[b, :TILE])
        lo_ref[b] = jnp.where(row < STEPS, q_ref[b, 2 * TILE :], low_ref[b])


def last_kernel(drift_ref, k_ref, mid_ref, lo_ref, hi_ref, rim_mid_ref, rim_hi_ref, product_ref, gram_ref):
    vectors, rows, cols = k_ref.shape
    total = DRIFT + rows
    by = lax.rem(drift_ref[0] + (total - DRIFT), total)
    for b in range(vectors):
        joined = jnp.concatenate(
            [rim_mid_ref[b], rim_hi_ref[b], lo_ref[b], mid_ref[b], hi_ref[b]], axis=0
        )
        product_ref[b] = k_ref[b] - pltpu.roll(joined, by, 0)[:rows]
    sums = []
    for a in range(vectors):
        for c in range(vectors):
            acc = jnp.sum((k_ref[a] * product_ref[c]).reshape(rows, cols // 128, 128), axis=1)
            sums.append(jnp.sum(acc, axis=0, keepdims=True))
    table = jnp.concatenate(sums, axis=0)
    ones = jnp.ones((gram_ref.shape[0], 128), jnp.float32)
    gram_ref[...] = lax.dot_general(
        ones, table, (((1,), (1,)), ((), ())),
        precision=lax.Precision.HIGHEST, preferred_element_type=jnp.float32,
    )


def call(kernel, outs, ins, scratch, flops):
    return pl.pallas_call(
        kernel,
        out_shape=[jax.ShapeDtypeStruct(o, jnp.float32) for o in outs],
        in_specs=ins,
        out_specs=[VMEM] * len(outs),
        scratch_shapes=[pltpu.VMEM(s, jnp.float32) for s in scratch],
        compiler_params=pltpu.CompilerParams(vmem_limit_bytes=LIMIT),
        cost_estimate=pl.CostEstimate(flops=flops, bytes_accessed=4 << 20, transcendentals=0),
    )


def body(krylov, advect_x, advect_y, step_counts, drifts):
    k, ax, ay = krylov[0], advect_x[0], advect_y[0]
    vectors, rows, cols = k.shape
    segs, strips = lax.axis_size("seg"), lax.axis_size("gx")
    fields = jnp.concatenate

    tail = fields([k[:, rows - STEPS :], ax[None, rows - STEPS :], ay[None, rows - STEPS :]], axis=0)
    head = fields([k[:, :STEPS], ax[None, :STEPS], ay[None, :STEPS]], axis=0)
    left = lax.ppermute(tail, "gx", shift_pairs(strips, 1))
    right = lax.ppermute(head, "gx", shift_pairs(strips, -1))
    drift = lax.ppermute(drifts, "seg", shift_pairs(segs, 1))

    flops = vectors * rows * cols * STEPS * 9
    mid, low, high = call(
        inner_kernel,
        [(vectors, rows - 2 * TILE, cols), (vectors, TILE, cols), (vectors, TILE, cols)],
        [SMEM, VMEM, VMEM, VMEM],
        [(vectors, rows, cols), (4, rows, cols)],
        flops,
    )(step_counts, k, ax, ay)
    onward = functools.partial(lax.ppermute, axis_name="seg", perm=shift_pairs(segs, 1))
    sideways = functools.partial(lax.ppermute, axis_name="gx", perm=shift_pairs(strips, 1))
    mid = onward(mid)
    lo, hi = call(
        outer_kernel,
        [(vectors, TILE, cols), (vectors, TILE, cols)],
        [SMEM] + [VMEM] * 7,
        [(vectors, 3 * TILE, cols), (4, 3 * TILE, cols)],
        flops,
    )(step_counts, k, ax, ay, left, right, low, high)
    hi = onward(hi)
    lo = onward(lo)
    rim_mid = sideways(mid[:, -(DRIFT - TILE) :])
    rim_hi = sideways(hi)
    world = segs * strips
    product, gram = call(
        last_kernel,
        [k.shape, (world, vectors * vectors)],
        [SMEM] + [VMEM] * 6,
        [],
        flops,
    )(drift, k, mid, lo, hi, rim_mid, rim_hi)
    gram = lax.all_to_all(gram, ("seg", "gx"), 0, 0)
    cells = world * rows * cols
    gram = jnp.sum(gram, axis=0).reshape(vectors, vectors) / jnp.float32(cells)
    return product[None], gram


def solution(mesh):
    return jax.shard_map(
        body,
        mesh=mesh,
        in_specs=(
            P("seg", None, "gx", None),
            P("seg", "gx", None),
            P("seg", "gx", None),
            P("seg"),
            P("seg"),
        ),
        out_specs=(P("seg", None, "gx", None), P()),
        check_vma=False,
    )
```

```python
import functools
import jax
import jax.numpy as jnp
from jax import lax
from jax.experimental import pallas as pl
from jax.experimental.pallas import tpu as pltpu
from jax.sharding import PartitionSpec as P

STEPS = 4
DRIFT = 16
TILE = 8

VMEM = pl.BlockSpec(memory_space=pltpu.VMEM)
SMEM = pl.BlockSpec(memory_space=pltpu.SMEM)
LIMIT = 32 * 1024 * 1024


def shift_pairs(count, by):
    return [(i, (i + by) % count) for i in range(count)]


def weights(ax, ay):
    col = lax.broadcasted_iota(jnp.int32, ax.shape, 1)
    last = ax.shape[1] - 1
    return (
        0.2 - ax,
        0.2 + ax,
        jnp.where(col == last, 0.0, 0.2 - ay),
        jnp.where(col == 0, 0.0, 0.2 + ay),
    )


def step(q, we, ww, wn, ws):
    rows, cols = q.shape
    return (
        0.2 * q
        + we * pltpu.roll(q, rows - 1, 0)
        + ww * pltpu.roll(q, 1, 0)
        + wn * pltpu.roll(q, cols - 1, 1)
        + ws * pltpu.roll(q, 1, 1)
    )


def inner_kernel(count_ref, k_ref, ax_ref, ay_ref, mid_ref, low_ref, high_ref, q_ref, w_ref):
    vectors, rows, _ = k_ref.shape
    for i, w in enumerate(weights(ax_ref[...], ay_ref[...])):
        w_ref[i] = w
    q_ref[...] = k_ref[...]

    @pl.loop(0, count_ref[0])
    def _(_):
        for b in range(vectors):
            q_ref[b] = step(q_ref[b], w_ref[0], w_ref[1], w_ref[2], w_ref[3])

    mid_ref[...] = q_ref[:, TILE : rows - TILE]
    low_ref[...] = q_ref[:, :TILE]
    high_ref[...] = q_ref[:, rows - TILE :]


def outer_kernel(
    count_ref, k_ref, ax_ref, ay_ref, left_ref, right_ref, low_ref, high_ref, lo_ref, hi_ref, q_ref, w_ref
):
    vectors, rows, _ = k_ref.shape

    def around(strip, at):
        return jnp.concatenate(
            [strip[rows - TILE :], right_ref[at], left_ref[at], strip[:TILE]], axis=0
        )

    for i, w in enumerate(weights(around(ax_ref, vectors), around(ay_ref, vectors + 1))):
        w_ref[i] = w
    for b in range(vectors):
        q_ref[b] = around(k_ref.at[b], b)

    @pl.loop(0, count_ref[0])
    def _(_):
        for b in range(vectors):
            q_ref[b] = step(q_ref[b], w_ref[0], w_ref[1], w_ref[2], w_ref[3])

    row = lax.broadcasted_iota(jnp.int32, lo_ref.shape[1:], 0)
    for b in range(vectors):
        hi_ref[b] = jnp.where(row < TILE - STEPS, high_ref[b], q_ref[b, :TILE])
        lo_ref[b] = jnp.where(row < STEPS, q_ref[b, 2 * TILE :], low_ref[b])


def pair_sums(left, right, blocks, vectors, cols):
    sums = []
    half = vectors // 2
    for first in range(0, vectors, half):
        accs = {}
        for block in range(blocks):
            for lane in range(0, cols, 128):
                rs = [right(c, block, lane) for c in range(vectors)]
                for a in range(first, first + half):
                    value = left(a, block, lane)
                    for c in range(vectors):
                        term = value * rs[c]
                        accs[a, c] = accs[a, c] + term if (a, c) in accs else term
        sums += [jnp.sum(accs[a, c], axis=0, keepdims=True) for a in range(first, first + half) for c in range(vectors)]
    return jnp.concatenate(sums, axis=0)


def tile_of(ref, v, block, lane):
    return ref[v, block * TILE : (block + 1) * TILE, lane : lane + 128]


def own_kernel(k_ref, table_ref):
    vectors, rows, cols = k_ref.shape
    tile = functools.partial(tile_of, k_ref)
    table_ref[...] = pair_sums(tile, tile, rows // TILE, vectors, cols)


def gram_kernel(drift_ref, k_ref, beyond_ref, lo_ref, mid_ref, hi_ref, own_ref, gram_ref, shifted_ref):
    vectors, rows, cols = k_ref.shape
    total = rows + beyond_ref.shape[1]
    by = lax.rem(total - drift_ref[0], total)
    for b in range(vectors):
        joined = jnp.concatenate([k_ref[b], beyond_ref[b]], axis=0)
        shifted_ref[b] = pltpu.roll(joined, by, 0)[:rows]
    blocks = rows // TILE

    def arrived(c, block, lane):
        if block == 0:
            return tile_of(lo_ref, c, 0, lane)
        if block == blocks - 1:
            return tile_of(hi_ref, c, 0, lane)
        return tile_of(mid_ref, c, block - 1, lane)

    table = own_ref[...] - pair_sums(functools.partial(tile_of, shifted_ref), arrived, blocks, vectors, cols)
    ones = jnp.ones((gram_ref.shape[0], 128), jnp.float32)
    gram_ref[...] = lax.dot_general(
        ones, table, (((1,), (1,)), ((), ())),
        precision=lax.Precision.HIGHEST, preferred_element_type=jnp.float32,
    )


def last_kernel(drift_ref, k_ref, mid_ref, lo_ref, hi_ref, rim_mid_ref, rim_hi_ref, product_ref):
    vectors, rows, _ = k_ref.shape
    total = DRIFT + rows
    by = lax.rem(drift_ref[0] + (total - DRIFT), total)
    for b in range(vectors):
        joined = jnp.concatenate(
            [rim_mid_ref[b], rim_hi_ref[b], lo_ref[b], mid_ref[b], hi_ref[b]], axis=0
        )
        product_ref[b] = k_ref[b] - pltpu.roll(joined, by, 0)[:rows]


def call(kernel, outs, ins, scratch, cost):
    return pl.pallas_call(
        kernel,
        out_shape=[jax.ShapeDtypeStruct(o, jnp.float32) for o in outs],
        in_specs=ins,
        out_specs=[VMEM] * len(outs),
        scratch_shapes=[pltpu.VMEM(s, jnp.float32) for s in scratch],
        compiler_params=pltpu.CompilerParams(vmem_limit_bytes=LIMIT),
        cost_estimate=pl.CostEstimate(flops=cost << 30, bytes_accessed=4 << 20, transcendentals=0),
    )


def body(krylov, advect_x, advect_y, step_counts, drifts):
    k, ax, ay = krylov[0], advect_x[0], advect_y[0]
    vectors, rows, cols = k.shape
    segs, strips = lax.axis_size("seg"), lax.axis_size("gx")
    fields = jnp.concatenate

    tail = fields([k[:, rows - STEPS :], ax[None, rows - STEPS :], ay[None, rows - STEPS :]], axis=0)
    head = fields([k[:, :STEPS], ax[None, :STEPS], ay[None, :STEPS]], axis=0)
    beyond = k[:, :DRIFT]
    tail, head, beyond, k, ax, ay = lax.optimization_barrier((tail, head, beyond, k, ax, ay))
    right = lax.ppermute(head, "gx", shift_pairs(strips, -1))
    left = lax.ppermute(tail, "gx", shift_pairs(strips, 1))
    drift = lax.ppermute(drifts, "seg", shift_pairs(segs, 1))
    beyond = lax.ppermute(beyond, "gx", shift_pairs(strips, -1))

    mid, low, high = call(
        inner_kernel,
        [(vectors, rows - 2 * TILE, cols), (vectors, TILE, cols), (vectors, TILE, cols)],
        [SMEM, VMEM, VMEM, VMEM],
        [(vectors, rows, cols), (4, rows, cols)],
        64,
    )(step_counts, k, ax, ay)
    onward = functools.partial(lax.ppermute, axis_name="seg", perm=shift_pairs(segs, 1))
    sideways = functools.partial(lax.ppermute, axis_name="gx", perm=shift_pairs(strips, 1))
    mid = onward(mid)
    lo, hi = call(
        outer_kernel,
        [(vectors, TILE, cols), (vectors, TILE, cols)],
        [SMEM] + [VMEM] * 7,
        [(vectors, 3 * TILE, cols), (4, 3 * TILE, cols)],
        64,
    )(step_counts, k, ax, ay, left, right, low, high)
    pairs = vectors * vectors
    hi, kept = lax.optimization_barrier((hi, k))
    hi = onward(hi)
    lo = onward(lo)
    (own,) = call(own_kernel, [(pairs, 128)], [VMEM], [], 4)(kept)
    rim_mid = sideways(mid[:, -(DRIFT - TILE) :])
    rim_hi = sideways(hi)
    world = segs * strips
    (gram,) = call(
        gram_kernel, [(world, pairs)], [SMEM] + [VMEM] * 6, [k.shape], 4
    )(drift, k, beyond, lo, mid, hi, own)
    gram = lax.all_to_all(gram, ("seg", "gx"), 0, 0)
    gram, rim_mid, rim_hi = lax.optimization_barrier((gram, rim_mid, rim_hi))
    (product,) = call(last_kernel, [k.shape], [SMEM] + [VMEM] * 6, [], 4)(
        drift, k, mid, lo, hi, rim_mid, rim_hi
    )
    cells = world * rows * cols
    gram = jnp.sum(gram, axis=0).reshape(vectors, vectors) / jnp.float32(cells)
    return product[None], gram


def solution(mesh):
    return jax.shard_map(
        body,
        mesh=mesh,
        in_specs=(
            P("seg", None, "gx", None),
            P("seg", "gx", None),
            P("seg", "gx", None),
            P("seg"),
            P("seg"),
        ),
        out_specs=(P("seg", None, "gx", None), P()),
        check_vma=False,
    )
```

```python
import functools
import jax
import jax.numpy as jnp
from jax import lax
from jax.experimental import pallas as pl
from jax.experimental.pallas import tpu as pltpu
from jax.sharding import PartitionSpec as P

STEPS = 4
DRIFT = 16
TILE = 8

ANY = pl.BlockSpec(memory_space=pl.ANY)
VMEM = pl.BlockSpec(memory_space=pltpu.VMEM)
SMEM = pl.BlockSpec(memory_space=pltpu.SMEM)
LIMIT = 32 * 1024 * 1024
FULL = 60 * 1024 * 1024


def shift_pairs(count, by):
    return [(i, (i + by) % count) for i in range(count)]


def weights(ax, ay):
    col = lax.broadcasted_iota(jnp.int32, ax.shape, 1)
    last = ax.shape[1] - 1
    return (
        0.2 - ax,
        0.2 + ax,
        jnp.where(col == last, 0.0, 0.2 - ay),
        jnp.where(col == 0, 0.0, 0.2 + ay),
    )


def step(q, we, ww, wn, ws):
    rows, cols = q.shape
    return (
        0.2 * q
        + we * pltpu.roll(q, rows - 1, 0)
        + ww * pltpu.roll(q, 1, 0)
        + wn * pltpu.roll(q, cols - 1, 1)
        + ws * pltpu.roll(q, 1, 1)
    )


def inner_kernel(
    count_ref, k_any, ax_any, ay_any,
    mid_ref, edge_ref, head_ref, tail_ref, beyond_ref,
    k_ref, a_ref, w_ref, sems,
):
    vectors, rows, _ = k_ref.shape
    copies = [
        pltpu.make_async_copy(source, target, sems.at[i])
        for i, (source, target) in enumerate(
            [(k_any.at[b], k_ref.at[b]) for b in range(vectors)]
            + [(ax_any, a_ref.at[0]), (ay_any, a_ref.at[1])]
        )
    ]
    for copy in copies[vectors:] + copies[:vectors]:
        copy.start()
    for i in range(2):
        copies[vectors + i].wait()
        head_ref[vectors + i] = a_ref[i, :STEPS]
        tail_ref[vectors + i] = a_ref[i, rows - STEPS :]
    for i, w in enumerate(weights(a_ref[0], a_ref[1])):
        w_ref[i] = w
    for b in range(vectors):
        copies[b].wait()
        q = lax.fori_loop(
            0, count_ref[0], lambda _, q: step(q, w_ref[0], w_ref[1], w_ref[2], w_ref[3]), k_ref[b]
        )
        mid_ref[b] = q[TILE : rows - TILE]
        edge_ref[b, :TILE] = q[:TILE]
        edge_ref[b, TILE:] = q[rows - TILE :]
        beyond_ref[b] = k_ref[b, :DRIFT]
        head_ref[b] = k_ref[b, :STEPS]
        tail_ref[b] = k_ref[b, rows - STEPS :]


def outer_kernel(
    count_ref, k_ref, ax_ref, ay_ref, left_ref, right_ref, edge_ref, lo_ref, hi_ref, w_ref
):
    vectors, rows, _ = k_ref.shape

    def around(strip, at):
        return jnp.concatenate(
            [strip[rows - TILE :], right_ref[at], left_ref[at], strip[:TILE]], axis=0
        )

    for i, w in enumerate(weights(around(ax_ref, vectors), around(ay_ref, vectors + 1))):
        w_ref[i] = w
    row = lax.broadcasted_iota(jnp.int32, lo_ref.shape[1:], 0)
    for b in range(vectors):
        q = lax.fori_loop(
            0, count_ref[0], lambda _, q: step(q, w_ref[0], w_ref[1], w_ref[2], w_ref[3]), around(k_ref.at[b], b)
        )
        hi_ref[b] = jnp.where(row < TILE - STEPS, edge_ref[b, TILE:], q[:TILE])
        lo_ref[b] = jnp.where(row < STEPS, q[2 * TILE :], edge_ref[b, :TILE])


def pair_sums(left, right, blocks, vectors, cols):
    sums = []
    half = vectors // 2
    for first in range(0, vectors, half):
        accs = {}
        for block in range(blocks):
            for lane in range(0, cols, 128):
                rs = [right(c, block, lane) for c in range(vectors)]
                for a in range(first, first + half):
                    value = left(a, block, lane)
                    for c in range(vectors):
                        term = value * rs[c]
                        accs[a, c] = accs[a, c] + term if (a, c) in accs else term
        sums += [jnp.sum(accs[a, c], axis=0, keepdims=True) for a in range(first, first + half) for c in range(vectors)]
    return jnp.concatenate(sums, axis=0)


def tile_of(ref, v, block, lane):
    return ref[v, block * TILE : (block + 1) * TILE, lane : lane + 128]


def own_kernel(drift_ref, k_ref, beyond_ref, table_ref, shifted_ref):
    vectors, rows, cols = k_ref.shape
    tile = functools.partial(tile_of, k_ref)
    table_ref[...] = pair_sums(tile, tile, rows // TILE, vectors, cols)
    total = rows + beyond_ref.shape[1]
    by = lax.rem(total - drift_ref[0], total)
    for b in range(vectors):
        joined = jnp.concatenate([k_ref[b], beyond_ref[b]], axis=0)
        shifted_ref[b] = pltpu.roll(joined, by, 0)[:rows]


def gram_kernel(shifted_ref, lo_ref, mid_ref, hi_ref, own_ref, gram_ref):
    vectors, rows, cols = shifted_ref.shape
    blocks = rows // TILE

    def arrived(c, block, lane):
        if block == 0:
            return tile_of(lo_ref, c, 0, lane)
        if block == blocks - 1:
            return tile_of(hi_ref, c, 0, lane)
        return tile_of(mid_ref, c, block - 1, lane)

    table = own_ref[...] - pair_sums(functools.partial(tile_of, shifted_ref), arrived, blocks, vectors, cols)
    ones = jnp.ones((gram_ref.shape[0], 128), jnp.float32)
    gram_ref[...] = lax.dot_general(
        ones, table, (((1,), (1,)), ((), ())),
        precision=lax.Precision.HIGHEST, preferred_element_type=jnp.float32,
    )


def last_kernel(drift_ref, k_ref, mid_ref, lo_ref, hi_ref, rim_mid_ref, rim_hi_ref, product_ref):
    vectors, rows, _ = k_ref.shape
    total = DRIFT + rows
    by = lax.rem(drift_ref[0] + (total - DRIFT), total)
    for b in range(vectors):
        joined = jnp.concatenate(
            [rim_mid_ref[b], rim_hi_ref[b], lo_ref[b], mid_ref[b], hi_ref[b]], axis=0
        )
        product_ref[b] = k_ref[b] - pltpu.roll(joined, by, 0)[:rows]


def buffer(*shape):
    return pltpu.VMEM(shape, jnp.float32)


def call(kernel, outs, ins, scratch, cost, limit=LIMIT):
    return pl.pallas_call(
        kernel,
        out_shape=[jax.ShapeDtypeStruct(o, jnp.float32) for o in outs],
        in_specs=ins,
        out_specs=[VMEM] * len(outs),
        scratch_shapes=scratch,
        compiler_params=pltpu.CompilerParams(vmem_limit_bytes=limit),
        cost_estimate=pl.CostEstimate(flops=cost << 30, bytes_accessed=4 << 20, transcendentals=0),
    )


def body(krylov, advect_x, advect_y, step_counts, drifts):
    k, ax, ay = krylov[0], advect_x[0], advect_y[0]
    vectors, rows, cols = k.shape
    segs, strips = lax.axis_size("seg"), lax.axis_size("gx")
    world, pairs = segs * strips, vectors * vectors
    fields = vectors + 2
    half = segs // 2
    onward = functools.partial(lax.ppermute, axis_name="seg", perm=shift_pairs(segs, 1))
    sideways = functools.partial(lax.ppermute, axis_name="gx", perm=shift_pairs(strips, 1))
    backward = functools.partial(lax.ppermute, axis_name="gx", perm=shift_pairs(strips, -1))

    mid, edge, head, tail, beyond = call(
        inner_kernel,
        [(vectors, rows - 2 * TILE, cols), (vectors, 2 * TILE, cols)]
        + [(fields, STEPS, cols)] * 2
        + [(vectors, DRIFT, cols)],
        [SMEM, ANY, ANY, ANY],
        [buffer(vectors, rows, cols), buffer(2, rows, cols), buffer(4, rows, cols), pltpu.SemaphoreType.DMA((fields,))],
        64,
        limit=FULL,
    )(step_counts, k, ax, ay)
    mid = lax.ppermute(mid, "seg", [(s, s // half * half + (s + 1) % half) for s in range(segs)])
    right = backward(head)
    left = sideways(tail)
    drift = onward(drifts)
    beyond = backward(beyond)
    lo, hi = call(
        outer_kernel,
        [(vectors, TILE, cols), (vectors, TILE, cols)],
        [SMEM] + [VMEM] * 6,
        [buffer(4, 3 * TILE, cols)],
        64,
    )(step_counts, k, ax, ay, left, right, edge)
    sent_lo, sent_hi, kept = lax.optimization_barrier((lo, hi, k))
    hi = onward(hi)
    lo = onward(lo)
    own, shifted = call(own_kernel, [(pairs, 128), k.shape], [SMEM, VMEM, VMEM], [], 4)(drift, kept, beyond)
    held, _, _ = lax.optimization_barrier((mid, sent_lo, sent_hi))
    crossed = lax.ppermute(held, "seg", [(0, half), (half, 0)])
    mid = jnp.where(lax.axis_index("seg") % half == 0, crossed, mid)
    rim_mid = sideways(mid[:, -(DRIFT - TILE) :])
    rim_hi = sideways(hi)
    (gram,) = call(gram_kernel, [(world, pairs)], [VMEM] * 5, [], 4)(shifted, lo, mid, hi, own)
    gram = lax.all_to_all(gram, ("seg", "gx"), 0, 0)
    (product,) = call(last_kernel, [k.shape], [SMEM] + [VMEM] * 6, [], 64)(
        drift, k, mid, lo, hi, rim_mid, rim_hi
    )
    product, gram = lax.optimization_barrier((product, gram))
    cells = world * rows * cols
    gram = jnp.sum(gram, axis=0).reshape(vectors, vectors) / jnp.float32(cells)
    return product[None], gram


def solution(mesh):
    return jax.shard_map(
        body,
        mesh=mesh,
        in_specs=(
            P("seg", None, "gx", None),
            P("seg", "gx", None),
            P("seg", "gx", None),
            P("seg"),
            P("seg"),
        ),
        out_specs=(P("seg", None, "gx", None), P()),
        check_vma=False,
    )
```

```python
import functools
import jax
import jax.numpy as jnp
from jax import lax
from jax.experimental import pallas as pl
from jax.experimental.pallas import tpu as pltpu
from jax.sharding import PartitionSpec as P

STEPS = 4
DRIFT = 16
TILE = 8

VMEM = pl.BlockSpec(memory_space=pltpu.VMEM)
SMEM = pl.BlockSpec(memory_space=pltpu.SMEM)
LIMIT = 12 * 1024 * 1024


def shift_pairs(count, by):
    return [(i, (i + by) % count) for i in range(count)]


def weights(ax, ay):
    col = lax.broadcasted_iota(jnp.int32, ax.shape, 1)
    last = ax.shape[1] - 1
    return (
        0.2 - ax,
        0.2 + ax,
        jnp.where(col == last, 0.0, 0.2 - ay),
        jnp.where(col == 0, 0.0, 0.2 + ay),
    )


def step(q, we, ww, wn, ws):
    rows, cols = q.shape
    return (
        0.2 * q
        + we * pltpu.roll(q, rows - 1, 0)
        + ww * pltpu.roll(q, 1, 0)
        + wn * pltpu.roll(q, cols - 1, 1)
        + ws * pltpu.roll(q, 1, 1)
    )


def inner_kernel(count_ref, k_ref, ax_ref, ay_ref, mid_ref, beyond_ref, q_ref, w_ref):
    vectors, rows, _ = k_ref.shape
    for i, w in enumerate(weights(ax_ref[...], ay_ref[...])):
        w_ref[i] = w
    q_ref[...] = k_ref[...]
    beyond_ref[...] = k_ref[:, :DRIFT]

    @pl.loop(0, count_ref[0])
    def _(_):
        for b in range(vectors):
            q_ref[b] = step(q_ref[b], w_ref[0], w_ref[1], w_ref[2], w_ref[3])

    mid_ref[...] = q_ref[:, TILE : rows - TILE]


def outer_kernel(count_ref, k_ref, ax_ref, ay_ref, left_ref, right_ref, out_ref, q_ref, w_ref):
    vectors, rows, _ = k_ref.shape

    def around(strip, at):
        return jnp.concatenate(
            [strip[rows - 2 * TILE :], right_ref[at], left_ref[at], strip[: 2 * TILE]], axis=0
        )

    for i, w in enumerate(weights(around(ax_ref, vectors), around(ay_ref, vectors + 1))):
        w_ref[i] = w
    for b in range(vectors):
        q_ref[b] = around(k_ref.at[b], b)

    @pl.loop(0, count_ref[0])
    def _(_):
        for b in range(vectors):
            q_ref[b] = step(q_ref[b], w_ref[0], w_ref[1], w_ref[2], w_ref[3])

    out_ref[:, :TILE] = q_ref[:, TILE : 2 * TILE]
    out_ref[:, TILE:] = q_ref[:, 3 * TILE : 4 * TILE]


def pair_sums(left, right, blocks, vectors, cols):
    sums = []
    half = vectors // 2
    for first in range(0, vectors, half):
        accs = {}
        for block in range(blocks):
            for lane in range(0, cols, 128):
                rs = [right(c, block, lane) for c in range(vectors)]
                for a in range(first, first + half):
                    value = left(a, block, lane)
                    for c in range(vectors):
                        term = value * rs[c]
                        accs[a, c] = accs[a, c] + term if (a, c) in accs else term
        sums += [jnp.sum(accs[a, c], axis=0, keepdims=True) for a in range(first, first + half) for c in range(vectors)]
    return jnp.concatenate(sums, axis=0)


def tile_of(ref, v, block, lane):
    return ref[v, block * TILE : (block + 1) * TILE, lane : lane + 128]


def own_kernel(drift_ref, k_ref, beyond_ref, table_ref, shifted_ref):
    vectors, rows, cols = k_ref.shape
    tile = functools.partial(tile_of, k_ref)
    table_ref[...] = pair_sums(tile, tile, rows // TILE, vectors, cols)
    total = rows + beyond_ref.shape[1]
    by = lax.rem(total - drift_ref[0], total)
    for b in range(vectors):
        joined = jnp.concatenate([k_ref[b], beyond_ref[b]], axis=0)
        shifted_ref[b] = pltpu.roll(joined, by, 0)[:rows]


def gram_kernel(shifted_ref, mid_ref, edge_ref, own_ref, gram_ref):
    vectors, rows, cols = shifted_ref.shape
    blocks = rows // TILE

    def arrived(c, block, lane):
        if block == 0:
            return tile_of(edge_ref, c, 1, lane)
        if block == blocks - 1:
            return tile_of(edge_ref, c, 0, lane)
        return tile_of(mid_ref, c, block - 1, lane)

    table = own_ref[...] - pair_sums(functools.partial(tile_of, shifted_ref), arrived, blocks, vectors, cols)
    ones = jnp.ones((gram_ref.shape[0], 128), jnp.float32)
    gram_ref[...] = lax.dot_general(
        ones, table, (((1,), (1,)), ((), ())),
        precision=lax.Precision.HIGHEST, preferred_element_type=jnp.float32,
    )


def last_kernel(drift_ref, k_ref, mid_ref, edge_ref, rim_mid_ref, rim_hi_ref, product_ref):
    vectors, rows, _ = k_ref.shape
    total = DRIFT + rows
    by = lax.rem(drift_ref[0] + (total - DRIFT), total)
    for b in range(vectors):
        joined = jnp.concatenate(
            [rim_mid_ref[b], rim_hi_ref[b], edge_ref[b, TILE:], mid_ref[b], edge_ref[b, :TILE]], axis=0
        )
        product_ref[b] = k_ref[b] - pltpu.roll(joined, by, 0)[:rows]


def buffer(*shape):
    return pltpu.VMEM(shape, jnp.float32)


def call(kernel, outs, ins, scratch, cost):
    return pl.pallas_call(
        kernel,
        out_shape=[jax.ShapeDtypeStruct(o, jnp.float32) for o in outs],
        in_specs=ins,
        out_specs=[VMEM] * len(outs),
        scratch_shapes=scratch,
        compiler_params=pltpu.CompilerParams(vmem_limit_bytes=LIMIT),
        cost_estimate=pl.CostEstimate(flops=cost << 30, bytes_accessed=4 << 20, transcendentals=0),
    )


def body(krylov, advect_x, advect_y, step_counts, drifts):
    k, ax, ay = krylov[0], advect_x[0], advect_y[0]
    vectors, rows, cols = k.shape
    segs, strips = lax.axis_size("seg"), lax.axis_size("gx")
    world, pairs = segs * strips, vectors * vectors
    half = segs // 2
    onward = functools.partial(lax.ppermute, axis_name="seg", perm=shift_pairs(segs, 1))
    sideways = functools.partial(lax.ppermute, axis_name="gx", perm=shift_pairs(strips, 1))
    backward = functools.partial(lax.ppermute, axis_name="gx", perm=shift_pairs(strips, -1))

    tail = jnp.concatenate([k[:, rows - STEPS :], ax[None, rows - STEPS :], ay[None, rows - STEPS :]], axis=0)
    head = jnp.concatenate([k[:, :STEPS], ax[None, :STEPS], ay[None, :STEPS]], axis=0)
    tail, head, k, ax, ay = lax.optimization_barrier((tail, head, k, ax, ay))
    right = backward(head)
    left = sideways(tail)
    drift = onward(drifts)
    mid, beyond = call(
        inner_kernel,
        [(vectors, rows - 2 * TILE, cols), (vectors, DRIFT, cols)],
        [SMEM, VMEM, VMEM, VMEM],
        [buffer(vectors, rows, cols), buffer(4, rows, cols)],
        64,
    )(step_counts, k, ax, ay)
    beyond, right = lax.optimization_barrier((beyond, right))
    beyond = backward(beyond)
    mid = lax.ppermute(mid, "seg", [(s, s // half * half + (s + 1) % half) for s in range(segs)])
    (edge,) = call(
        outer_kernel,
        [(vectors, 2 * TILE, cols)],
        [SMEM] + [VMEM] * 5,
        [buffer(vectors, 5 * TILE, cols), buffer(4, 5 * TILE, cols)],
        1,
    )(step_counts, k, ax, ay, left, right)
    sent, kept = lax.optimization_barrier((edge, k))
    edge = onward(edge)
    own, shifted = call(own_kernel, [(pairs, 128), k.shape], [SMEM, VMEM, VMEM], [], 16)(drift, kept, beyond)
    held, _ = lax.optimization_barrier((mid, sent))
    crossed = lax.ppermute(held, "seg", [(0, half), (half, 0)])
    mid = jnp.where(lax.axis_index("seg") % half == 0, crossed, mid)
    rim_mid = sideways(mid[:, -(DRIFT - TILE) :])
    edge, own, _ = lax.optimization_barrier((edge, own, mid))
    rim_hi = sideways(edge[:, :TILE])
    (gram,) = call(gram_kernel, [(world, pairs)], [VMEM] * 4, [], 1)(shifted, mid, edge, own)
    gram = lax.all_to_all(gram, ("seg", "gx"), 0, 0)
    (product,) = call(last_kernel, [k.shape], [SMEM] + [VMEM] * 5, [], 1)(
        drift, k, mid, edge, rim_mid, rim_hi
    )
    product, gram = lax.optimization_barrier((product, gram))
    cells = world * rows * cols
    gram = jnp.sum(gram, axis=0).reshape(vectors, vectors) / jnp.float32(cells)
    return product[None], gram


def solution(mesh):
    return jax.shard_map(
        body,
        mesh=mesh,
        in_specs=(
            P("seg", None, "gx", None),
            P("seg", "gx", None),
            P("seg", "gx", None),
            P("seg"),
            P("seg"),
        ),
        out_specs=(P("seg", None, "gx", None), P()),
        check_vma=False,
    )
```

```python
import functools
import jax
import jax.numpy as jnp
from jax import lax
from jax.experimental import pallas as pl
from jax.experimental.pallas import tpu as pltpu
from jax.sharding import PartitionSpec as P

STEPS = 4
DRIFT = 16
TILE = 8

ANY = pl.BlockSpec(memory_space=pl.ANY)
VMEM = pl.BlockSpec(memory_space=pltpu.VMEM)
SMEM = pl.BlockSpec(memory_space=pltpu.SMEM)
LIMIT = 12 * 1024 * 1024
FULL = 60 * 1024 * 1024


def shift_pairs(count, by):
    return [(i, (i + by) % count) for i in range(count)]


def weights(ax, ay):
    col = lax.broadcasted_iota(jnp.int32, ax.shape, 1)
    last = ax.shape[1] - 1
    return (
        0.2 - ax,
        0.2 + ax,
        jnp.where(col == last, 0.0, 0.2 - ay),
        jnp.where(col == 0, 0.0, 0.2 + ay),
    )


def step(q, we, ww, wn, ws):
    rows, cols = q.shape
    return (
        0.2 * q
        + we * pltpu.roll(q, rows - 1, 0)
        + ww * pltpu.roll(q, 1, 0)
        + wn * pltpu.roll(q, cols - 1, 1)
        + ws * pltpu.roll(q, 1, 1)
    )


def pack_kernel(k_any, ax_any, ay_any, head_ref, tail_ref, low_ref, high_ref, sems):
    rows = k_any.shape[1]
    vectors = k_any.shape[0]
    copies = []
    for i, (at, target) in enumerate(((0, low_ref), (rows - TILE, high_ref))):
        copies += [
            pltpu.make_async_copy(k_any.at[:, pl.ds(at, TILE)], target.at[pl.ds(0, vectors)], sems.at[i, 0]),
            pltpu.make_async_copy(ax_any.at[pl.ds(at, TILE)], target.at[vectors], sems.at[i, 1]),
            pltpu.make_async_copy(ay_any.at[pl.ds(at, TILE)], target.at[vectors + 1], sems.at[i, 2]),
        ]
    for copy in copies:
        copy.start()
    for copy in copies:
        copy.wait()
    head_ref[...] = low_ref[:, :STEPS]
    tail_ref[...] = high_ref[:, TILE - STEPS :]


def inner_kernel(count_ref, k_ref, ax_ref, ay_ref, mid_ref, q_ref, w_ref):
    vectors, rows, _ = k_ref.shape
    for i, w in enumerate(weights(ax_ref[...], ay_ref[...])):
        w_ref[i] = w
    q_ref[...] = k_ref[...]

    @pl.loop(0, count_ref[0])
    def _(_):
        for b in range(vectors):
            q_ref[b] = step(q_ref[b], w_ref[0], w_ref[1], w_ref[2], w_ref[3])

    mid_ref[...] = q_ref[:, TILE : rows - TILE]


def outer_kernel(count_ref, k_ref, ax_ref, ay_ref, left_ref, right_ref, mid_ref, lo_ref, hi_ref, upper_ref, q_ref, w_ref):
    vectors, rows, _ = k_ref.shape

    def around(strip, at):
        return jnp.concatenate(
            [strip[rows - 2 * TILE :], right_ref[at], left_ref[at], strip[: 2 * TILE]], axis=0
        )

    for i, w in enumerate(weights(around(ax_ref, vectors), around(ay_ref, vectors + 1))):
        w_ref[i] = w
    for b in range(vectors):
        q_ref[b] = around(k_ref.at[b], b)

    @pl.loop(0, count_ref[0])
    def _(_):
        for b in range(vectors):
            q_ref[b] = step(q_ref[b], w_ref[0], w_ref[1], w_ref[2], w_ref[3])

    hi_ref[...] = q_ref[:, TILE : 2 * TILE]
    lo_ref[...] = q_ref[:, 3 * TILE : 4 * TILE]
    upper_ref[:, :TILE] = mid_ref[:, TILE:]
    upper_ref[:, TILE:] = q_ref[:, TILE : 2 * TILE]


def pair_sums(left, right, blocks, vectors, cols):
    sums = []
    half = vectors // 2
    for first in range(0, vectors, half):
        accs = {}
        for block in range(blocks):
            for lane in range(0, cols, 128):
                rs = [right(c, block, lane) for c in range(vectors)]
                for a in range(first, first + half):
                    value = left(a, block, lane)
                    for c in range(vectors):
                        term = value * rs[c]
                        accs[a, c] = accs[a, c] + term if (a, c) in accs else term
        sums += [jnp.sum(accs[a, c], axis=0, keepdims=True) for a in range(first, first + half) for c in range(vectors)]
    return jnp.concatenate(sums, axis=0)


def tile_of(ref, v, block, lane):
    return ref[v, block * TILE : (block + 1) * TILE, lane : lane + 128]


def last_kernel(
    drift_ref, k_ref, mid_ref, lo_ref, hi_ref, rim_mid_ref, rim_hi_ref, upper_ref, product_any, gram_ref, product_ref, sems
):
    vectors, rows, cols = k_ref.shape
    total = DRIFT + rows
    by = lax.rem(drift_ref[0] + (total - DRIFT), total)
    copies = [pltpu.make_async_copy(product_ref.at[b], product_any.at[b], sems.at[b]) for b in range(vectors)]
    for b in range(vectors):
        joined = jnp.concatenate(
            [
                rim_mid_ref[b] + upper_ref[b, :TILE],
                rim_hi_ref[b] + upper_ref[b, TILE:],
                lo_ref[b],
                mid_ref[b],
                hi_ref[b],
            ],
            axis=0,
        )
        product_ref[b] = k_ref[b] - pltpu.roll(joined, by, 0)[:rows]
        copies[b].start()
    table = pair_sums(
        functools.partial(tile_of, k_ref), functools.partial(tile_of, product_ref), rows // TILE, vectors, cols
    )
    ones = jnp.ones((gram_ref.shape[0], 128), jnp.float32)
    gram_ref[...] = lax.dot_general(
        ones, table, (((1,), (1,)), ((), ())),
        precision=lax.Precision.HIGHEST, preferred_element_type=jnp.float32,
    )
    for copy in copies:
        copy.wait()


def buffer(*shape):
    return pltpu.VMEM(shape, jnp.float32)


def call(kernel, outs, ins, scratch, cost, limit=LIMIT, places=None):
    return pl.pallas_call(
        kernel,
        out_shape=[jax.ShapeDtypeStruct(o, jnp.float32) for o in outs],
        in_specs=ins,
        out_specs=places or [VMEM] * len(outs),
        scratch_shapes=scratch,
        compiler_params=pltpu.CompilerParams(vmem_limit_bytes=limit),
        cost_estimate=pl.CostEstimate(flops=cost << 30, bytes_accessed=4 << 20, transcendentals=0),
    )


def rim_pairs(segs, strips, direct):
    pairs = []
    for s in range(segs):
        for g in range(strips):
            busy = (s + 1) % (segs // 2) == 0 and g % 2 == 1
            if busy == direct:
                pairs.append(((s - direct) * strips + g, s * strips + (g + 1) % strips))
    return pairs


def body(krylov, advect_x, advect_y, step_counts, drifts):
    k, ax, ay = krylov[0], advect_x[0], advect_y[0]
    vectors, rows, cols = k.shape
    segs, strips = lax.axis_size("seg"), lax.axis_size("gx")
    world, pairs = segs * strips, vectors * vectors
    fields = vectors + 2
    onward = functools.partial(lax.ppermute, axis_name="seg", perm=shift_pairs(segs, 1))
    sideways = functools.partial(lax.ppermute, axis_name=("seg", "gx"), perm=rim_pairs(segs, strips, False))
    ahead = functools.partial(lax.ppermute, axis_name=("seg", "gx"), perm=rim_pairs(segs, strips, True))

    head, tail = call(
        pack_kernel,
        [(fields, STEPS, cols)] * 2,
        [ANY] * 3,
        [buffer(fields, TILE, cols), buffer(fields, TILE, cols), pltpu.SemaphoreType.DMA((2, 3))],
        1,
        limit=FULL,
    )(k, ax, ay)
    right = lax.ppermute(head, "gx", shift_pairs(strips, -1))
    left = lax.ppermute(tail, "gx", shift_pairs(strips, 1))
    drift = onward(drifts)
    (mid,) = call(
        inner_kernel,
        [(vectors, rows - 2 * TILE, cols)],
        [SMEM, VMEM, VMEM, VMEM],
        [buffer(vectors, rows, cols), buffer(4, rows, cols)],
        64,
    )(step_counts, k, ax, ay)
    lo, hi, upper = call(
        outer_kernel,
        [(vectors, TILE, cols), (vectors, TILE, cols), (vectors, 2 * TILE, cols)],
        [SMEM] + [VMEM] * 6,
        [buffer(vectors, 5 * TILE, cols), buffer(4, 5 * TILE, cols)],
        1,
    )(step_counts, k, ax, ay, left, right, mid)
    mid = onward(mid)
    hi = onward(hi)
    lo = onward(lo)
    upper = ahead(upper)
    near = mid[:, -(DRIFT - TILE) :]
    rim_mid = sideways(near)
    rim_hi = sideways(lax.optimization_barrier((hi, near))[0])
    product, gram = call(
        last_kernel,
        [k.shape, (world, pairs)],
        [SMEM] + [VMEM] * 7,
        [buffer(*k.shape), pltpu.SemaphoreType.DMA((vectors,))],
        1,
        places=[ANY, VMEM],
    )(drift, k, mid, lo, hi, rim_mid, rim_hi, upper)
    gram = lax.all_to_all(gram, ("seg", "gx"), 0, 0)
    cells = world * rows * cols
    gram = jnp.sum(gram, axis=0).reshape(vectors, vectors) / jnp.float32(cells)
    return product[None], gram


def solution(mesh):
    return jax.shard_map(
        body,
        mesh=mesh,
        in_specs=(
            P("seg", None, "gx", None),
            P("seg", "gx", None),
            P("seg", "gx", None),
            P("seg"),
            P("seg"),
        ),
        out_specs=(P("seg", None, "gx", None), P()),
        check_vma=False,
    )
```

```python
import functools
import jax
import jax.numpy as jnp
from jax import lax
from jax.experimental import pallas as pl
from jax.experimental.pallas import tpu as pltpu
from jax.sharding import PartitionSpec as P

STEPS = 4
DRIFT = 16
TILE = 8

ANY = pl.BlockSpec(memory_space=pl.ANY)
VMEM = pl.BlockSpec(memory_space=pltpu.VMEM)
SMEM = pl.BlockSpec(memory_space=pltpu.SMEM)
LIMIT = 12 * 1024 * 1024
FULL = 60 * 1024 * 1024


def shift_pairs(count, by):
    return [(i, (i + by) % count) for i in range(count)]


def weights(ax, ay):
    col = lax.broadcasted_iota(jnp.int32, ax.shape, 1)
    last = ax.shape[1] - 1
    return (
        0.2 - ax,
        0.2 + ax,
        jnp.where(col == last, 0.0, 0.2 - ay),
        jnp.where(col == 0, 0.0, 0.2 + ay),
    )


def step(q, we, ww, wn, ws):
    rows, cols = q.shape
    return (
        0.2 * q
        + we * pltpu.roll(q, rows - 1, 0)
        + ww * pltpu.roll(q, 1, 0)
        + wn * pltpu.roll(q, cols - 1, 1)
        + ws * pltpu.roll(q, 1, 1)
    )


def inner_kernel(
    count_ref, k_any, ax_any, ay_any, mid_any, beyond_any, head_ref, tail_ref, k_ref, a_ref, q_ref, w_ref, sems, out_sems
):
    vectors, rows, _ = k_ref.shape
    half = vectors // 2
    groups = [pl.ds(0, half), pl.ds(half, vectors - half)]
    copies = [
        pltpu.make_async_copy(ax_any, a_ref.at[0], sems.at[0]),
        pltpu.make_async_copy(ay_any, a_ref.at[1], sems.at[1]),
    ] + [pltpu.make_async_copy(k_any.at[group], k_ref.at[group], sems.at[2 + i]) for i, group in enumerate(groups)]
    beyond = pltpu.make_async_copy(k_any.at[:, pl.ds(0, DRIFT)], beyond_any, out_sems.at[2])
    for copy in copies:
        copy.start()
    beyond.start()
    for i in range(2):
        copies[i].wait()
        head_ref[vectors + i] = a_ref[i, :STEPS]
        tail_ref[vectors + i] = a_ref[i, rows - STEPS :]
    for i, w in enumerate(weights(a_ref[0], a_ref[1])):
        w_ref[i] = w
    outs = []
    for i, group in enumerate(groups):
        copies[2 + i].wait()
        first, size = group.start, group.size
        head_ref[first : first + size] = k_ref[first : first + size, :STEPS]
        tail_ref[first : first + size] = k_ref[first : first + size, rows - STEPS :]
        q_ref[first : first + size] = k_ref[first : first + size]

        @pl.loop(0, count_ref[0])
        def _(_):
            for b in range(first, first + size):
                q_ref[b] = step(q_ref[b], w_ref[0], w_ref[1], w_ref[2], w_ref[3])

        outs.append(
            pltpu.make_async_copy(q_ref.at[group, pl.ds(TILE, rows - 2 * TILE)], mid_any.at[group], out_sems.at[i])
        )
        outs[i].start()
    for copy in outs + [beyond]:
        copy.wait()


def outer_kernel(count_ref, k_ref, ax_ref, ay_ref, left_ref, right_ref, lo_ref, hi_ref, table_ref, q_ref, w_ref):
    vectors, rows, _ = k_ref.shape

    def around(strip, at):
        return jnp.concatenate(
            [strip[rows - 2 * TILE :], right_ref[at], left_ref[at], strip[: 2 * TILE]], axis=0
        )

    for i, w in enumerate(weights(around(ax_ref, vectors), around(ay_ref, vectors + 1))):
        w_ref[i] = w
    for b in range(vectors):
        q_ref[b] = around(k_ref.at[b], b)

    @pl.loop(0, count_ref[0])
    def _(_):
        for b in range(vectors):
            q_ref[b] = step(q_ref[b], w_ref[0], w_ref[1], w_ref[2], w_ref[3])

    hi_ref[...] = q_ref[:, TILE : 2 * TILE]
    lo_ref[...] = q_ref[:, 3 * TILE : 4 * TILE]
    tile = functools.partial(tile_of, k_ref)
    table_ref[...] = pair_sums(tile, tile, rows // TILE, vectors, k_ref.shape[2])


def pair_sums(left, right, blocks, vectors, cols):
    sums = []
    half = vectors // 2
    for first in range(0, vectors, half):
        accs = {}
        for block in range(blocks):
            for lane in range(0, cols, 128):
                rs = [right(c, block, lane) for c in range(vectors)]
                for a in range(first, first + half):
                    value = left(a, block, lane)
                    for c in range(vectors):
                        term = value * rs[c]
                        accs[a, c] = accs[a, c] + term if (a, c) in accs else term
        sums += [jnp.sum(accs[a, c], axis=0, keepdims=True) for a in range(first, first + half) for c in range(vectors)]
    return jnp.concatenate(sums, axis=0)


def tile_of(ref, v, block, lane):
    return ref[v, block * TILE : (block + 1) * TILE, lane : lane + 128]


def gram_kernel(
    drift_ref, k_ref, beyond_ref, lo_ref, mid_ref, hi_ref, upper_ref, own_ref, gram_ref, shifted_ref, before_ref
):
    vectors, rows, cols = k_ref.shape
    drift = drift_ref[0]
    blocks = rows // TILE
    total = rows + DRIFT
    back = lax.rem(total - drift, total)
    row = lax.broadcasted_iota(jnp.int32, (DRIFT, cols), 0)
    for b in range(vectors):
        joined = jnp.concatenate([k_ref[b], beyond_ref[b]], axis=0)
        shifted_ref[b] = pltpu.roll(joined, back, 0)[:rows]
        before_ref[b] = jnp.where(row < drift, pltpu.roll(upper_ref[b], lax.rem(drift, DRIFT), 0), 0.0)

    def left(a, block, lane):
        if block < blocks:
            return tile_of(shifted_ref, a, block, lane)
        return tile_of(k_ref, a, block - blocks, lane)

    def right(c, block, lane):
        if block == 0:
            return tile_of(lo_ref, c, 0, lane)
        if block < blocks - 1:
            return tile_of(mid_ref, c, block - 1, lane)
        if block == blocks - 1:
            return tile_of(hi_ref, c, 0, lane)
        return tile_of(before_ref, c, block - blocks, lane)

    table = own_ref[...] - pair_sums(left, right, blocks + DRIFT // TILE, vectors, cols)
    ones = jnp.ones((gram_ref.shape[0], 128), jnp.float32)
    gram_ref[...] = lax.dot_general(
        ones, table, (((1,), (1,)), ((), ())),
        precision=lax.Precision.HIGHEST, preferred_element_type=jnp.float32,
    )


def last_kernel(drift_ref, k_ref, mid_ref, lo_ref, hi_ref, rim_mid_ref, rim_hi_ref, upper_ref, product_ref):
    vectors, rows, _ = k_ref.shape
    total = DRIFT + rows
    by = lax.rem(drift_ref[0] + (total - DRIFT), total)
    for b in range(vectors):
        joined = jnp.concatenate(
            [
                rim_mid_ref[b] + upper_ref[b, :TILE],
                rim_hi_ref[b] + upper_ref[b, TILE:],
                lo_ref[b],
                mid_ref[b],
                hi_ref[b],
            ],
            axis=0,
        )
        product_ref[b] = k_ref[b] - pltpu.roll(joined, by, 0)[:rows]


def buffer(*shape):
    return pltpu.VMEM(shape, jnp.float32)


def call(kernel, outs, ins, scratch, cost, limit=LIMIT, places=None):
    return pl.pallas_call(
        kernel,
        out_shape=[jax.ShapeDtypeStruct(o, jnp.float32) for o in outs],
        in_specs=ins,
        out_specs=places or [VMEM] * len(outs),
        scratch_shapes=scratch,
        compiler_params=pltpu.CompilerParams(vmem_limit_bytes=limit),
        cost_estimate=pl.CostEstimate(flops=cost << 30, bytes_accessed=cost << 20, transcendentals=0),
    )


def rim_pairs(segs, strips, direct):
    pairs = []
    for s in range(segs):
        for g in range(strips):
            busy = (s + 1) % (segs // 2) == 0 and g % 2 == 1
            if busy == direct:
                pairs.append(((s - direct) * strips + g, s * strips + (g + 1) % strips))
    return pairs


def body(krylov, advect_x, advect_y, step_counts, drifts):
    k, ax, ay = krylov[0], advect_x[0], advect_y[0]
    vectors, rows, cols = k.shape
    segs, strips = lax.axis_size("seg"), lax.axis_size("gx")
    world, pairs = segs * strips, vectors * vectors
    fields = vectors + 2
    onward = functools.partial(lax.ppermute, axis_name="seg", perm=shift_pairs(segs, 1))
    along = rim_pairs(segs, strips, False)
    sideways = functools.partial(lax.ppermute, axis_name=("seg", "gx"), perm=along)
    backward = functools.partial(lax.ppermute, axis_name=("seg", "gx"), perm=[(b, a) for a, b in along])
    ahead = functools.partial(lax.ppermute, axis_name=("seg", "gx"), perm=rim_pairs(segs, strips, True))

    mid, beyond, head, tail = call(
        inner_kernel,
        [(vectors, rows - 2 * TILE, cols), (vectors, DRIFT, cols)] + [(fields, STEPS, cols)] * 2,
        [SMEM, ANY, ANY, ANY],
        [
            buffer(vectors, rows, cols),
            buffer(2, rows, cols),
            buffer(vectors, rows, cols),
            buffer(4, rows, cols),
            pltpu.SemaphoreType.DMA((4,)),
            pltpu.SemaphoreType.DMA((3,)),
        ],
        64,
        limit=FULL,
        places=[ANY, ANY, VMEM, VMEM],
    )(step_counts, k, ax, ay)
    right = lax.ppermute(head, "gx", shift_pairs(strips, -1))
    left = lax.ppermute(tail, "gx", shift_pairs(strips, 1))
    drift = onward(drifts)
    lo, hi, own = call(
        outer_kernel,
        [(vectors, TILE, cols), (vectors, TILE, cols), (pairs, 128)],
        [SMEM] + [VMEM] * 5,
        [buffer(vectors, 5 * TILE, cols), buffer(4, 5 * TILE, cols)],
        0,
    )(step_counts, k, ax, ay, left, right)
    upper = ahead(jnp.concatenate([mid[:, -(DRIFT - TILE) :], hi], axis=1))
    beyond = backward(beyond)
    mid = onward(mid)
    hi = onward(hi)
    lo = onward(lo)
    near = mid[:, -(DRIFT - TILE) :]
    rim_mid = sideways(near)
    rim_hi = sideways(lax.optimization_barrier((hi, near))[0])
    (gram,) = call(
        gram_kernel,
        [(world, pairs)],
        [SMEM] + [VMEM] * 7,
        [buffer(*k.shape), buffer(vectors, DRIFT, cols)],
        1,
    )(drift, k, beyond, lo, mid, hi, upper, own)
    gram = lax.all_to_all(gram, ("seg", "gx"), 0, 0)
    (product,) = call(last_kernel, [k.shape], [SMEM] + [VMEM] * 7, [], 1)(
        drift, k, mid, lo, hi, rim_mid, rim_hi, upper
    )
    product, gram = lax.optimization_barrier((product, gram))
    cells = world * rows * cols
    gram = jnp.sum(gram, axis=0).reshape(vectors, vectors) / jnp.float32(cells)
    return product[None], gram


def solution(mesh):
    return jax.shard_map(
        body,
        mesh=mesh,
        in_specs=(
            P("seg", None, "gx", None),
            P("seg", "gx", None),
            P("seg", "gx", None),
            P("seg"),
            P("seg"),
        ),
        out_specs=(P("seg", None, "gx", None), P()),
        check_vma=False,
    )
```

```python
import functools
import jax
import jax.numpy as jnp
from jax import lax
from jax.experimental import pallas as pl
from jax.experimental.pallas import tpu as pltpu
from jax.sharding import PartitionSpec as P

STEPS = 4
DRIFT = 16
TILE = 8

ANY = pl.BlockSpec(memory_space=pl.ANY)
VMEM = pl.BlockSpec(memory_space=pltpu.VMEM)
SMEM = pl.BlockSpec(memory_space=pltpu.SMEM)
LIMIT = 12 * 1024 * 1024
FULL = 60 * 1024 * 1024


def shift_pairs(count, by):
    return [(i, (i + by) % count) for i in range(count)]


def weights(ax, ay):
    col = lax.broadcasted_iota(jnp.int32, ax.shape, 1)
    last = ax.shape[1] - 1
    return (
        0.2 - ax,
        0.2 + ax,
        jnp.where(col == last, 0.0, 0.2 - ay),
        jnp.where(col == 0, 0.0, 0.2 + ay),
    )


def step(q, we, ww, wn, ws):
    rows, cols = q.shape
    return (
        0.2 * q
        + we * pltpu.roll(q, rows - 1, 0)
        + ww * pltpu.roll(q, 1, 0)
        + wn * pltpu.roll(q, cols - 1, 1)
        + ws * pltpu.roll(q, 1, 1)
    )


def inner_kernel(
    count_ref, k_any, ax_any, ay_any, mid_any, beyond_any, head_ref, tail_ref, k_ref, a_ref, q_ref, w_ref, sems, out_sems
):
    vectors, rows, _ = k_ref.shape
    half = vectors // 2
    groups = [pl.ds(0, half), pl.ds(half, vectors - half)]
    copies = [
        pltpu.make_async_copy(ax_any, a_ref.at[0], sems.at[0]),
        pltpu.make_async_copy(ay_any, a_ref.at[1], sems.at[1]),
    ] + [pltpu.make_async_copy(k_any.at[group], k_ref.at[group], sems.at[2 + i]) for i, group in enumerate(groups)]
    for copy in copies:
        copy.start()
    for i in range(2):
        copies[i].wait()
        head_ref[vectors + i] = a_ref[i, :STEPS]
        tail_ref[vectors + i] = a_ref[i, rows - STEPS :]
    for i, w in enumerate(weights(a_ref[0], a_ref[1])):
        w_ref[i] = w
    outs = []
    for i, group in enumerate(groups):
        copies[2 + i].wait()
        first, size = group.start, group.size
        head_ref[first : first + size] = k_ref[first : first + size, :STEPS]
        tail_ref[first : first + size] = k_ref[first : first + size, rows - STEPS :]
        q_ref[first : first + size] = k_ref[first : first + size]

        @pl.loop(0, count_ref[0])
        def _(_):
            for b in range(first, first + size):
                q_ref[b] = step(q_ref[b], w_ref[0], w_ref[1], w_ref[2], w_ref[3])

        outs.append(
            pltpu.make_async_copy(q_ref.at[group, pl.ds(TILE, rows - 2 * TILE)], mid_any.at[group], out_sems.at[i])
        )
        outs[i].start()
    outs.append(pltpu.make_async_copy(k_ref.at[:, pl.ds(0, DRIFT)], beyond_any, out_sems.at[2]))
    outs[-1].start()
    for copy in outs:
        copy.wait()


def outer_kernel(count_ref, k_ref, ax_ref, ay_ref, left_ref, right_ref, edge_ref, table_ref, q_ref, w_ref):
    vectors, rows, _ = k_ref.shape

    def around(strip, at):
        return jnp.concatenate(
            [strip[rows - 2 * TILE :], right_ref[at], left_ref[at], strip[: 2 * TILE]], axis=0
        )

    for i, w in enumerate(weights(around(ax_ref, vectors), around(ay_ref, vectors + 1))):
        w_ref[i] = w
    for b in range(vectors):
        q_ref[b] = around(k_ref.at[b], b)

    @pl.loop(0, count_ref[0])
    def _(_):
        for b in range(vectors):
            q_ref[b] = step(q_ref[b], w_ref[0], w_ref[1], w_ref[2], w_ref[3])

    edge_ref[:, :TILE] = q_ref[:, TILE : 2 * TILE]
    edge_ref[:, TILE:] = q_ref[:, 3 * TILE : 4 * TILE]
    tile = functools.partial(tile_of, k_ref)
    table_ref[...] = pair_sums(tile, tile, rows // TILE, vectors, k_ref.shape[2])


def pair_sums(left, right, blocks, vectors, cols):
    sums = []
    half = vectors // 2
    for first in range(0, vectors, half):
        accs = {}
        for block in range(blocks):
            for lane in range(0, cols, 128):
                rs = [right(c, block, lane) for c in range(vectors)]
                for a in range(first, first + half):
                    value = left(a, block, lane)
                    for c in range(vectors):
                        term = value * rs[c]
                        accs[a, c] = accs[a, c] + term if (a, c) in accs else term
        sums += [jnp.sum(accs[a, c], axis=0, keepdims=True) for a in range(first, first + half) for c in range(vectors)]
    return jnp.concatenate(sums, axis=0)


def tile_of(ref, v, block, lane):
    return ref[v, block * TILE : (block + 1) * TILE, lane : lane + 128]


def gram_kernel(
    drift_ref, k_ref, beyond_ref, mid_ref, edge_ref, upper_ref, own_ref, gram_ref, shifted_ref, before_ref
):
    vectors, rows, cols = k_ref.shape
    drift = drift_ref[0]
    blocks = rows // TILE
    total = rows + DRIFT
    back = lax.rem(total - drift, total)
    row = lax.broadcasted_iota(jnp.int32, (DRIFT, cols), 0)
    for b in range(vectors):
        joined = jnp.concatenate([k_ref[b], beyond_ref[b]], axis=0)
        shifted_ref[b] = pltpu.roll(joined, back, 0)[:rows]
        before_ref[b] = jnp.where(row < drift, pltpu.roll(upper_ref[b], lax.rem(drift, DRIFT), 0), 0.0)

    def left(a, block, lane):
        if block < blocks:
            return tile_of(shifted_ref, a, block, lane)
        return tile_of(k_ref, a, block - blocks, lane)

    def right(c, block, lane):
        if block == 0:
            return tile_of(edge_ref, c, 1, lane)
        if block < blocks - 1:
            return tile_of(mid_ref, c, block - 1, lane)
        if block == blocks - 1:
            return tile_of(edge_ref, c, 0, lane)
        return tile_of(before_ref, c, block - blocks, lane)

    table = own_ref[...] - pair_sums(left, right, blocks + DRIFT // TILE, vectors, cols)
    ones = jnp.ones((gram_ref.shape[0], 128), jnp.float32)
    gram_ref[...] = lax.dot_general(
        ones, table, (((1,), (1,)), ((), ())),
        precision=lax.Precision.HIGHEST, preferred_element_type=jnp.float32,
    )


def last_kernel(drift_ref, k_ref, mid_ref, edge_ref, rim_ref, upper_ref, product_ref):
    vectors, rows, _ = k_ref.shape
    total = DRIFT + rows
    by = lax.rem(drift_ref[0] + (total - DRIFT), total)
    for b in range(vectors):
        joined = jnp.concatenate(
            [rim_ref[b] + upper_ref[b], edge_ref[b, TILE:], mid_ref[b], edge_ref[b, :TILE]], axis=0
        )
        product_ref[b] = k_ref[b] - pltpu.roll(joined, by, 0)[:rows]


def buffer(*shape):
    return pltpu.VMEM(shape, jnp.float32)


def call(kernel, outs, ins, scratch, cost, limit=LIMIT, places=None):
    return pl.pallas_call(
        kernel,
        out_shape=[jax.ShapeDtypeStruct(o, jnp.float32) for o in outs],
        in_specs=ins,
        out_specs=places or [VMEM] * len(outs),
        scratch_shapes=scratch,
        compiler_params=pltpu.CompilerParams(vmem_limit_bytes=limit),
        cost_estimate=pl.CostEstimate(flops=cost << 30, bytes_accessed=cost << 20, transcendentals=0),
    )


def rim_pairs(segs, strips, direct):
    pairs = []
    for s in range(segs):
        for g in range(strips):
            busy = (s + 1) % (segs // 2) == 0 and g % 2 == 1
            if busy == direct:
                pairs.append(((s - direct) * strips + g, s * strips + (g + 1) % strips))
    return pairs


def body(krylov, advect_x, advect_y, step_counts, drifts):
    k, ax, ay = krylov[0], advect_x[0], advect_y[0]
    vectors, rows, cols = k.shape
    segs, strips = lax.axis_size("seg"), lax.axis_size("gx")
    world, pairs = segs * strips, vectors * vectors
    fields = vectors + 2
    onward = functools.partial(lax.ppermute, axis_name="seg", perm=shift_pairs(segs, 1))
    along = rim_pairs(segs, strips, False)
    sideways = functools.partial(lax.ppermute, axis_name=("seg", "gx"), perm=along)
    backward = functools.partial(lax.ppermute, axis_name=("seg", "gx"), perm=[(b, a) for a, b in along])
    ahead = functools.partial(lax.ppermute, axis_name=("seg", "gx"), perm=rim_pairs(segs, strips, True))

    mid, beyond, head, tail = call(
        inner_kernel,
        [(vectors, rows - 2 * TILE, cols), (vectors, DRIFT, cols)] + [(fields, STEPS, cols)] * 2,
        [SMEM, ANY, ANY, ANY],
        [
            buffer(vectors, rows, cols),
            buffer(2, rows, cols),
            buffer(vectors, rows, cols),
            buffer(4, rows, cols),
            pltpu.SemaphoreType.DMA((4,)),
            pltpu.SemaphoreType.DMA((3,)),
        ],
        64,
        limit=FULL,
        places=[ANY, ANY, VMEM, VMEM],
    )(step_counts, k, ax, ay)
    right = lax.ppermute(head, "gx", shift_pairs(strips, -1))
    left = lax.ppermute(tail, "gx", shift_pairs(strips, 1))
    drift = onward(drifts)
    edge, own = call(
        outer_kernel,
        [(vectors, 2 * TILE, cols), (pairs, 128)],
        [SMEM] + [VMEM] * 5,
        [buffer(vectors, 5 * TILE, cols), buffer(4, 5 * TILE, cols)],
        0,
    )(step_counts, k, ax, ay, left, right)
    upper = ahead(jnp.concatenate([mid[:, -(DRIFT - TILE) :], edge[:, :TILE]], axis=1))
    beyond = backward(beyond)
    mid = onward(mid)
    edge = onward(edge)
    (gram,) = call(
        gram_kernel,
        [(world, pairs)],
        [SMEM] + [VMEM] * 6,
        [buffer(*k.shape), buffer(vectors, DRIFT, cols)],
        1,
    )(drift, k, beyond, mid, edge, upper, own)
    near, gram = lax.optimization_barrier((jnp.concatenate([mid[:, -(DRIFT - TILE) :], edge[:, :TILE]], axis=1), gram))
    rim = sideways(near)
    gram = lax.all_to_all(gram, ("seg", "gx"), 0, 0)
    (product,) = call(last_kernel, [k.shape], [SMEM] + [VMEM] * 5, [], 1)(
        drift, k, mid, edge, rim, upper
    )
    product, gram = lax.optimization_barrier((product, gram))
    cells = world * rows * cols
    gram = jnp.sum(gram, axis=0).reshape(vectors, vectors) / jnp.float32(cells)
    return product[None], gram


def solution(mesh):
    return jax.shard_map(
        body,
        mesh=mesh,
        in_specs=(
            P("seg", None, "gx", None),
            P("seg", "gx", None),
            P("seg", "gx", None),
            P("seg"),
            P("seg"),
        ),
        out_specs=(P("seg", None, "gx", None), P()),
        check_vma=False,
    )
```

```python
import functools
import jax
import jax.numpy as jnp
from jax import lax
from jax.experimental import pallas as pl
from jax.experimental.pallas import tpu as pltpu
from jax.sharding import PartitionSpec as P

STEPS = 4
DRIFT = 16
TILE = 8

ANY = pl.BlockSpec(memory_space=pl.ANY)
VMEM = pl.BlockSpec(memory_space=pltpu.VMEM)
SMEM = pl.BlockSpec(memory_space=pltpu.SMEM)
LIMIT = 12 * 1024 * 1024
FULL = 60 * 1024 * 1024


def shift_pairs(count, by):
    return [(i, (i + by) % count) for i in range(count)]


def weights(ax, ay):
    col = lax.broadcasted_iota(jnp.int32, ax.shape, 1)
    last = ax.shape[1] - 1
    return (
        0.2 - ax,
        0.2 + ax,
        jnp.where(col == last, 0.0, 0.2 - ay),
        jnp.where(col == 0, 0.0, 0.2 + ay),
    )


def step(q, we, ww, wn, ws):
    rows, cols = q.shape
    return (
        0.2 * q
        + we * pltpu.roll(q, rows - 1, 0)
        + ww * pltpu.roll(q, 1, 0)
        + wn * pltpu.roll(q, cols - 1, 1)
        + ws * pltpu.roll(q, 1, 1)
    )


def inner_kernel(
    count_ref, k_any, ax_any, ay_any, mid_any, beyond_any, head_ref, tail_ref, k_ref, a_ref, q_ref, w_ref, sems, out_sems
):
    vectors, rows, _ = k_ref.shape
    half = vectors // 2
    groups = [pl.ds(0, half), pl.ds(half, vectors - half)]
    copies = [
        pltpu.make_async_copy(ax_any, a_ref.at[0], sems.at[0]),
        pltpu.make_async_copy(ay_any, a_ref.at[1], sems.at[1]),
    ] + [pltpu.make_async_copy(k_any.at[group], k_ref.at[group], sems.at[2 + i]) for i, group in enumerate(groups)]
    for copy in copies:
        copy.start()
    for i in range(2):
        copies[i].wait()
        head_ref[vectors + i] = a_ref[i, :STEPS]
        tail_ref[vectors + i] = a_ref[i, rows - STEPS :]
    for i, w in enumerate(weights(a_ref[0], a_ref[1])):
        w_ref[i] = w
    outs = []
    for i, group in enumerate(groups):
        copies[2 + i].wait()
        first, size = group.start, group.size
        head_ref[first : first + size] = k_ref[first : first + size, :STEPS]
        tail_ref[first : first + size] = k_ref[first : first + size, rows - STEPS :]
        q_ref[first : first + size] = k_ref[first : first + size]

        @pl.loop(0, count_ref[0])
        def _(_):
            for b in range(first, first + size):
                q_ref[b] = step(q_ref[b], w_ref[0], w_ref[1], w_ref[2], w_ref[3])

        outs.append(
            pltpu.make_async_copy(q_ref.at[group, pl.ds(TILE, rows - 2 * TILE)], mid_any.at[group], out_sems.at[i])
        )
        outs[i].start()
    outs.append(pltpu.make_async_copy(k_ref.at[:, pl.ds(0, DRIFT)], beyond_any, out_sems.at[2]))
    outs[-1].start()
    for copy in outs:
        copy.wait()


def outer_kernel(count_ref, k_ref, ax_ref, ay_ref, left_ref, right_ref, edge_ref, table_ref, q_ref, w_ref):
    vectors, rows, _ = k_ref.shape

    def around(strip, at):
        return jnp.concatenate(
            [strip[rows - 2 * TILE :], right_ref[at], left_ref[at], strip[: 2 * TILE]], axis=0
        )

    for i, w in enumerate(weights(around(ax_ref, vectors), around(ay_ref, vectors + 1))):
        w_ref[i] = w
    for b in range(vectors):
        q_ref[b] = around(k_ref.at[b], b)

    @pl.loop(0, count_ref[0])
    def _(_):
        for b in range(vectors):
            q_ref[b] = step(q_ref[b], w_ref[0], w_ref[1], w_ref[2], w_ref[3])

    edge_ref[:, :TILE] = q_ref[:, TILE : 2 * TILE]
    edge_ref[:, TILE:] = q_ref[:, 3 * TILE : 4 * TILE]
    tile = functools.partial(tile_of, k_ref)
    table_ref[...] = pair_sums(tile, tile, rows // TILE, vectors, k_ref.shape[2])


def pair_sums(left, right, blocks, vectors, cols):
    sums = []
    half = vectors // 2
    for first in range(0, vectors, half):
        accs = {}
        for block in range(blocks):
            for lane in range(0, cols, 128):
                rs = [right(c, block, lane) for c in range(vectors)]
                for a in range(first, first + half):
                    value = left(a, block, lane)
                    for c in range(vectors):
                        term = value * rs[c]
                        accs[a, c] = accs[a, c] + term if (a, c) in accs else term
        sums += [jnp.sum(accs[a, c], axis=0, keepdims=True) for a in range(first, first + half) for c in range(vectors)]
    return jnp.concatenate(sums, axis=0)


def tile_of(ref, v, block, lane):
    return ref[v, block * TILE : (block + 1) * TILE, lane : lane + 128]


def gram_kernel(
    drift_ref, k_ref, beyond_ref, mid_ref, edge_ref, upper_ref, own_ref, gram_ref, near_ref, shifted_ref, before_ref
):
    vectors, rows, cols = k_ref.shape
    drift = drift_ref[0]
    blocks = rows // TILE
    near_ref[:, : DRIFT - TILE] = mid_ref[:, -(DRIFT - TILE) :]
    near_ref[:, DRIFT - TILE :] = edge_ref[:, :TILE]
    total = rows + DRIFT
    back = lax.rem(total - drift, total)
    row = lax.broadcasted_iota(jnp.int32, (DRIFT, cols), 0)
    for b in range(vectors):
        joined = jnp.concatenate([k_ref[b], beyond_ref[b]], axis=0)
        shifted_ref[b] = pltpu.roll(joined, back, 0)[:rows]
        before_ref[b] = jnp.where(row < drift, pltpu.roll(upper_ref[b], lax.rem(drift, DRIFT), 0), 0.0)

    def left(a, block, lane):
        if block < blocks:
            return tile_of(shifted_ref, a, block, lane)
        return tile_of(k_ref, a, block - blocks, lane)

    def right(c, block, lane):
        if block == 0:
            return tile_of(edge_ref, c, 1, lane)
        if block < blocks - 1:
            return tile_of(mid_ref, c, block - 1, lane)
        if block == blocks - 1:
            return tile_of(edge_ref, c, 0, lane)
        return tile_of(before_ref, c, block - blocks, lane)

    table = own_ref[...] - pair_sums(left, right, blocks + DRIFT // TILE, vectors, cols)
    ones = jnp.ones((gram_ref.shape[0], 128), jnp.float32)
    gram_ref[...] = lax.dot_general(
        ones, table, (((1,), (1,)), ((), ())),
        precision=lax.Precision.HIGHEST, preferred_element_type=jnp.float32,
    )


def last_kernel(drift_ref, k_ref, mid_ref, edge_ref, rim_ref, upper_ref, product_ref):
    vectors, rows, _ = k_ref.shape
    total = DRIFT + rows
    by = lax.rem(drift_ref[0] + (total - DRIFT), total)
    for b in range(vectors):
        joined = jnp.concatenate(
            [rim_ref[b] + upper_ref[b], edge_ref[b, TILE:], mid_ref[b], edge_ref[b, :TILE]], axis=0
        )
        product_ref[b] = k_ref[b] - pltpu.roll(joined, by, 0)[:rows]


def buffer(*shape):
    return pltpu.VMEM(shape, jnp.float32)


def call(kernel, outs, ins, scratch, cost, limit=LIMIT, places=None):
    return pl.pallas_call(
        kernel,
        out_shape=[jax.ShapeDtypeStruct(o, jnp.float32) for o in outs],
        in_specs=ins,
        out_specs=places or [VMEM] * len(outs),
        scratch_shapes=scratch,
        compiler_params=pltpu.CompilerParams(vmem_limit_bytes=limit),
        cost_estimate=pl.CostEstimate(flops=cost << 30, bytes_accessed=cost << 20, transcendentals=0),
    )


def rim_pairs(segs, strips, direct):
    pairs = []
    for s in range(segs):
        for g in range(strips):
            crosses = g % 2 == 1 and s != segs // 2
            if crosses == direct:
                pairs.append((((s - direct) % segs) * strips + g, s * strips + (g + 1) % strips))
    return pairs


def body(krylov, advect_x, advect_y, step_counts, drifts):
    k, ax, ay = krylov[0], advect_x[0], advect_y[0]
    vectors, rows, cols = k.shape
    segs, strips = lax.axis_size("seg"), lax.axis_size("gx")
    world, pairs = segs * strips, vectors * vectors
    fields = vectors + 2
    onward = functools.partial(lax.ppermute, axis_name="seg", perm=shift_pairs(segs, 1))
    along = rim_pairs(segs, strips, False)
    sideways = functools.partial(lax.ppermute, axis_name=("seg", "gx"), perm=along)
    backward = functools.partial(lax.ppermute, axis_name=("seg", "gx"), perm=[(b, a) for a, b in along])
    ahead = functools.partial(lax.ppermute, axis_name=("seg", "gx"), perm=rim_pairs(segs, strips, True))

    mid, beyond, head, tail = call(
        inner_kernel,
        [(vectors, rows - 2 * TILE, cols), (vectors, DRIFT, cols)] + [(fields, STEPS, cols)] * 2,
        [SMEM, ANY, ANY, ANY],
        [
            buffer(vectors, rows, cols),
            buffer(2, rows, cols),
            buffer(vectors, rows, cols),
            buffer(4, rows, cols),
            pltpu.SemaphoreType.DMA((4,)),
            pltpu.SemaphoreType.DMA((3,)),
        ],
        64,
        limit=FULL,
        places=[ANY, ANY, VMEM, VMEM],
    )(step_counts, k, ax, ay)
    right = lax.ppermute(head, "gx", shift_pairs(strips, -1))
    left = lax.ppermute(tail, "gx", shift_pairs(strips, 1))
    drift = onward(drifts)
    edge, own = call(
        outer_kernel,
        [(vectors, 2 * TILE, cols), (pairs, 128)],
        [SMEM] + [VMEM] * 5,
        [buffer(vectors, 5 * TILE, cols), buffer(4, 5 * TILE, cols)],
        0,
    )(step_counts, k, ax, ay, left, right)
    upper = ahead(jnp.concatenate([mid[:, -(DRIFT - TILE) :], edge[:, :TILE]], axis=1))
    beyond = backward(beyond)
    mid = onward(mid)
    edge = onward(edge)
    gram, near = call(
        gram_kernel,
        [(world, pairs), (vectors, DRIFT, cols)],
        [SMEM] + [VMEM] * 6,
        [buffer(*k.shape), buffer(vectors, DRIFT, cols)],
        1,
    )(drift, k, beyond, mid, edge, upper, own)
    rim = sideways(near)
    gram = lax.all_to_all(gram, ("seg", "gx"), 0, 0)
    (product,) = call(last_kernel, [k.shape], [SMEM] + [VMEM] * 5, [], 1)(
        drift, k, mid, edge, rim, upper
    )
    product, gram = lax.optimization_barrier((product, gram))
    cells = world * rows * cols
    gram = jnp.sum(gram, axis=0).reshape(vectors, vectors) / jnp.float32(cells)
    return product[None], gram


def solution(mesh):
    return jax.shard_map(
        body,
        mesh=mesh,
        in_specs=(
            P("seg", None, "gx", None),
            P("seg", "gx", None),
            P("seg", "gx", None),
            P("seg"),
            P("seg"),
        ),
        out_specs=(P("seg", None, "gx", None), P()),
        check_vma=False,
    )
```

```python
import functools
import jax
import jax.numpy as jnp
from jax import lax
from jax.experimental import pallas as pl
from jax.experimental.pallas import tpu as pltpu
from jax.sharding import PartitionSpec as P

STEPS = 4
DRIFT = 16
TILE = 8

ANY = pl.BlockSpec(memory_space=pl.ANY)
VMEM = pl.BlockSpec(memory_space=pltpu.VMEM)
SMEM = pl.BlockSpec(memory_space=pltpu.SMEM)
LIMIT = 12 * 1024 * 1024
FULL = 60 * 1024 * 1024


def shift_pairs(count, by):
    return [(i, (i + by) % count) for i in range(count)]


def weights(ax, ay):
    col = lax.broadcasted_iota(jnp.int32, ax.shape, 1)
    last = ax.shape[1] - 1
    return (
        0.2 - ax,
        0.2 + ax,
        jnp.where(col == last, 0.0, 0.2 - ay),
        jnp.where(col == 0, 0.0, 0.2 + ay),
    )


def step(q, we, ww, wn, ws):
    rows, cols = q.shape
    return (
        0.2 * q
        + we * pltpu.roll(q, rows - 1, 0)
        + ww * pltpu.roll(q, 1, 0)
        + wn * pltpu.roll(q, cols - 1, 1)
        + ws * pltpu.roll(q, 1, 1)
    )


def pack_kernel(k_any, ax_any, ay_any, head_ref, tail_ref, low_ref, high_ref, sems):
    rows = k_any.shape[1]
    vectors = k_any.shape[0]
    copies = []
    for i, (at, target) in enumerate(((0, low_ref), (rows - TILE, high_ref))):
        copies += [
            pltpu.make_async_copy(k_any.at[:, pl.ds(at, TILE)], target.at[pl.ds(0, vectors)], sems.at[i, 0]),
            pltpu.make_async_copy(ax_any.at[pl.ds(at, TILE)], target.at[vectors], sems.at[i, 1]),
            pltpu.make_async_copy(ay_any.at[pl.ds(at, TILE)], target.at[vectors + 1], sems.at[i, 2]),
        ]
    for copy in copies:
        copy.start()
    for copy in copies:
        copy.wait()
    head_ref[...] = low_ref[:, :STEPS]
    tail_ref[...] = high_ref[:, TILE - STEPS :]


def inner_kernel(count_ref, k_ref, ax_ref, ay_ref, mid_ref, beyond_ref, q_ref, w_ref):
    vectors, rows, _ = k_ref.shape
    for i, w in enumerate(weights(ax_ref[...], ay_ref[...])):
        w_ref[i] = w
    q_ref[...] = k_ref[...]

    @pl.loop(0, count_ref[0])
    def _(_):
        for b in range(vectors):
            q_ref[b] = step(q_ref[b], w_ref[0], w_ref[1], w_ref[2], w_ref[3])

    mid_ref[...] = q_ref[:, TILE : rows - TILE]
    beyond_ref[...] = k_ref[:, :DRIFT]


def outer_kernel(count_ref, k_ref, ax_ref, ay_ref, left_ref, right_ref, edge_ref, table_ref, q_ref, w_ref):
    vectors, rows, _ = k_ref.shape

    def around(strip, at):
        return jnp.concatenate(
            [strip[rows - 2 * TILE :], right_ref[at], left_ref[at], strip[: 2 * TILE]], axis=0
        )

    for i, w in enumerate(weights(around(ax_ref, vectors), around(ay_ref, vectors + 1))):
        w_ref[i] = w
    for b in range(vectors):
        q_ref[b] = around(k_ref.at[b], b)

    @pl.loop(0, count_ref[0])
    def _(_):
        for b in range(vectors):
            q_ref[b] = step(q_ref[b], w_ref[0], w_ref[1], w_ref[2], w_ref[3])

    edge_ref[:, :TILE] = q_ref[:, TILE : 2 * TILE]
    edge_ref[:, TILE:] = q_ref[:, 3 * TILE : 4 * TILE]
    tile = functools.partial(tile_of, k_ref)
    table_ref[...] = pair_sums(tile, tile, rows // TILE, vectors, k_ref.shape[2])


def pair_sums(left, right, blocks, vectors, cols):
    sums = []
    half = vectors // 2
    for first in range(0, vectors, half):
        accs = {}
        for block in range(blocks):
            for lane in range(0, cols, 128):
                rs = [right(c, block, lane) for c in range(vectors)]
                for a in range(first, first + half):
                    value = left(a, block, lane)
                    for c in range(vectors):
                        term = value * rs[c]
                        accs[a, c] = accs[a, c] + term if (a, c) in accs else term
        sums += [jnp.sum(accs[a, c], axis=0, keepdims=True) for a in range(first, first + half) for c in range(vectors)]
    return jnp.concatenate(sums, axis=0)


def tile_of(ref, v, block, lane):
    return ref[v, block * TILE : (block + 1) * TILE, lane : lane + 128]


def gram_kernel(
    drift_ref, k_ref, beyond_ref, mid_ref, edge_ref, upper_ref, own_ref, gram_ref, near_ref, shifted_ref, before_ref
):
    vectors, rows, cols = k_ref.shape
    drift = drift_ref[0]
    blocks = rows // TILE
    near_ref[:, : DRIFT - TILE] = mid_ref[:, -(DRIFT - TILE) :]
    near_ref[:, DRIFT - TILE :] = edge_ref[:, :TILE]
    total = rows + DRIFT
    back = lax.rem(total - drift, total)
    row = lax.broadcasted_iota(jnp.int32, (DRIFT, cols), 0)
    for b in range(vectors):
        joined = jnp.concatenate([k_ref[b], beyond_ref[b]], axis=0)
        shifted_ref[b] = pltpu.roll(joined, back, 0)[:rows]
        before_ref[b] = jnp.where(row < drift, pltpu.roll(upper_ref[b], lax.rem(drift, DRIFT), 0), 0.0)

    def left(a, block, lane):
        if block < blocks:
            return tile_of(shifted_ref, a, block, lane)
        return tile_of(k_ref, a, block - blocks, lane)

    def right(c, block, lane):
        if block == 0:
            return tile_of(edge_ref, c, 1, lane)
        if block < blocks - 1:
            return tile_of(mid_ref, c, block - 1, lane)
        if block == blocks - 1:
            return tile_of(edge_ref, c, 0, lane)
        return tile_of(before_ref, c, block - blocks, lane)

    table = own_ref[...] - pair_sums(left, right, blocks + DRIFT // TILE, vectors, cols)
    ones = jnp.ones((gram_ref.shape[0], 128), jnp.float32)
    gram_ref[...] = lax.dot_general(
        ones, table, (((1,), (1,)), ((), ())),
        precision=lax.Precision.HIGHEST, preferred_element_type=jnp.float32,
    )


def last_kernel(drift_ref, k_ref, mid_ref, edge_ref, rim_ref, upper_ref, product_ref):
    vectors, rows, _ = k_ref.shape
    total = DRIFT + rows
    by = lax.rem(drift_ref[0] + (total - DRIFT), total)
    for b in range(vectors):
        joined = jnp.concatenate(
            [rim_ref[b] + upper_ref[b], edge_ref[b, TILE:], mid_ref[b], edge_ref[b, :TILE]], axis=0
        )
        product_ref[b] = k_ref[b] - pltpu.roll(joined, by, 0)[:rows]


def buffer(*shape):
    return pltpu.VMEM(shape, jnp.float32)


def call(kernel, outs, ins, scratch, cost, limit=LIMIT):
    return pl.pallas_call(
        kernel,
        out_shape=[jax.ShapeDtypeStruct(o, jnp.float32) for o in outs],
        in_specs=ins,
        out_specs=[VMEM] * len(outs),
        scratch_shapes=scratch,
        compiler_params=pltpu.CompilerParams(vmem_limit_bytes=limit),
        cost_estimate=pl.CostEstimate(flops=cost << 30, bytes_accessed=cost << 20, transcendentals=0),
    )


def rim_pairs(segs, strips, direct):
    pairs = []
    for s in range(segs):
        for g in range(strips):
            crosses = g % 2 == 1 and s != segs // 2
            if crosses == direct:
                pairs.append((((s - direct) % segs) * strips + g, s * strips + (g + 1) % strips))
    return pairs


def body(krylov, advect_x, advect_y, step_counts, drifts):
    k, ax, ay = krylov[0], advect_x[0], advect_y[0]
    vectors, rows, cols = k.shape
    segs, strips = lax.axis_size("seg"), lax.axis_size("gx")
    world, pairs = segs * strips, vectors * vectors
    fields = vectors + 2
    onward = functools.partial(lax.ppermute, axis_name="seg", perm=shift_pairs(segs, 1))
    along = rim_pairs(segs, strips, False)
    sideways = functools.partial(lax.ppermute, axis_name=("seg", "gx"), perm=along)
    backward = functools.partial(lax.ppermute, axis_name=("seg", "gx"), perm=[(b, a) for a, b in along])
    ahead = functools.partial(lax.ppermute, axis_name=("seg", "gx"), perm=rim_pairs(segs, strips, True))

    head, tail = call(
        pack_kernel,
        [(fields, STEPS, cols)] * 2,
        [ANY] * 3,
        [buffer(fields, TILE, cols), buffer(fields, TILE, cols), pltpu.SemaphoreType.DMA((2, 3))],
        1,
        limit=FULL,
    )(k, ax, ay)
    right = lax.ppermute(head, "gx", shift_pairs(strips, -1))
    left = lax.ppermute(tail, "gx", shift_pairs(strips, 1))
    mid, beyond = call(
        inner_kernel,
        [(vectors, rows - 2 * TILE, cols), (vectors, DRIFT, cols)],
        [SMEM, VMEM, VMEM, VMEM],
        [buffer(vectors, rows, cols), buffer(4, rows, cols)],
        64,
    )(step_counts, k, ax, ay)
    drift = onward(drifts)
    edge, own = call(
        outer_kernel,
        [(vectors, 2 * TILE, cols), (pairs, 128)],
        [SMEM] + [VMEM] * 5,
        [buffer(vectors, 5 * TILE, cols), buffer(4, 5 * TILE, cols)],
        0,
    )(step_counts, k, ax, ay, left, right)
    upper = ahead(jnp.concatenate([mid[:, -(DRIFT - TILE) :], edge[:, :TILE]], axis=1))
    beyond, _ = lax.optimization_barrier((beyond, edge))
    beyond = backward(beyond)
    mid = onward(mid)
    edge = onward(edge)
    gram, near = call(
        gram_kernel,
        [(world, pairs), (vectors, DRIFT, cols)],
        [SMEM] + [VMEM] * 6,
        [buffer(*k.shape), buffer(vectors, DRIFT, cols)],
        1,
    )(drift, k, beyond, mid, edge, upper, own)
    rim = sideways(near)
    gram = lax.all_to_all(gram, ("seg", "gx"), 0, 0)
    (product,) = call(last_kernel, [k.shape], [SMEM] + [VMEM] * 5, [], 1)(
        drift, k, mid, edge, rim, upper
    )
    product, gram = lax.optimization_barrier((product, gram))
    cells = world * rows * cols
    gram = jnp.sum(gram, axis=0).reshape(vectors, vectors) / jnp.float32(cells)
    return product[None], gram


def solution(mesh):
    return jax.shard_map(
        body,
        mesh=mesh,
        in_specs=(
            P("seg", None, "gx", None),
            P("seg", "gx", None),
            P("seg", "gx", None),
            P("seg"),
            P("seg"),
        ),
        out_specs=(P("seg", None, "gx", None), P()),
        check_vma=False,
    )
```

```python
import functools
import jax
import jax.numpy as jnp
from jax import lax
from jax.experimental import pallas as pl
from jax.experimental.pallas import tpu as pltpu
from jax.sharding import PartitionSpec as P

STEPS = 4
DRIFT = 16
TILE = 8

ANY = pl.BlockSpec(memory_space=pl.ANY)
VMEM = pl.BlockSpec(memory_space=pltpu.VMEM)
SMEM = pl.BlockSpec(memory_space=pltpu.SMEM)
LIMIT = 12 * 1024 * 1024
FULL = 60 * 1024 * 1024


def shift_pairs(count, by):
    return [(i, (i + by) % count) for i in range(count)]


def weights(ax, ay):
    col = lax.broadcasted_iota(jnp.int32, ax.shape, 1)
    last = ax.shape[1] - 1
    return (
        0.2 - ax,
        0.2 + ax,
        jnp.where(col == last, 0.0, 0.2 - ay),
        jnp.where(col == 0, 0.0, 0.2 + ay),
    )


def step(q, we, ww, wn, ws):
    rows, cols = q.shape
    return (
        0.2 * q
        + we * pltpu.roll(q, rows - 1, 0)
        + ww * pltpu.roll(q, 1, 0)
        + wn * pltpu.roll(q, cols - 1, 1)
        + ws * pltpu.roll(q, 1, 1)
    )


def pack_kernel(k_any, ax_any, ay_any, head_ref, tail_ref, low_ref, high_ref, sems):
    rows = k_any.shape[1]
    vectors = k_any.shape[0]
    copies = []
    for i, (at, target) in enumerate(((0, low_ref), (rows - TILE, high_ref))):
        copies += [
            pltpu.make_async_copy(k_any.at[:, pl.ds(at, TILE)], target.at[pl.ds(0, vectors)], sems.at[i, 0]),
            pltpu.make_async_copy(ax_any.at[pl.ds(at, TILE)], target.at[vectors], sems.at[i, 1]),
            pltpu.make_async_copy(ay_any.at[pl.ds(at, TILE)], target.at[vectors + 1], sems.at[i, 2]),
        ]
    for copy in copies:
        copy.start()
    for copy in copies:
        copy.wait()
    head_ref[...] = low_ref[:, :STEPS]
    tail_ref[...] = high_ref[:, TILE - STEPS :]


def inner_kernel(count_ref, k_ref, ax_ref, ay_ref, mid_ref, beyond_ref, q_ref, w_ref):
    vectors, rows, _ = k_ref.shape
    for i, w in enumerate(weights(ax_ref[...], ay_ref[...])):
        w_ref[i] = w
    q_ref[...] = k_ref[...]
    beyond_ref[...] = k_ref[:, :DRIFT]

    @pl.loop(0, count_ref[0])
    def _(_):
        for b in range(vectors):
            q_ref[b] = step(q_ref[b], w_ref[0], w_ref[1], w_ref[2], w_ref[3])

    mid_ref[...] = q_ref[:, TILE : rows - TILE]


def outer_kernel(count_ref, k_ref, ax_ref, ay_ref, left_ref, right_ref, out_ref, q_ref, w_ref):
    vectors, rows, _ = k_ref.shape

    def around(strip, at):
        return jnp.concatenate(
            [strip[rows - 2 * TILE :], right_ref[at], left_ref[at], strip[: 2 * TILE]], axis=0
        )

    for i, w in enumerate(weights(around(ax_ref, vectors), around(ay_ref, vectors + 1))):
        w_ref[i] = w
    for b in range(vectors):
        q_ref[b] = around(k_ref.at[b], b)

    @pl.loop(0, count_ref[0])
    def _(_):
        for b in range(vectors):
            q_ref[b] = step(q_ref[b], w_ref[0], w_ref[1], w_ref[2], w_ref[3])

    out_ref[:, :TILE] = q_ref[:, TILE : 2 * TILE]
    out_ref[:, TILE:] = q_ref[:, 3 * TILE : 4 * TILE]


def pair_sums(left, right, blocks, vectors, cols):
    sums = []
    half = vectors // 2
    for first in range(0, vectors, half):
        accs = {}
        for block in range(blocks):
            for lane in range(0, cols, 128):
                rs = [right(c, block, lane) for c in range(vectors)]
                for a in range(first, first + half):
                    value = left(a, block, lane)
                    for c in range(vectors):
                        term = value * rs[c]
                        accs[a, c] = accs[a, c] + term if (a, c) in accs else term
        sums += [jnp.sum(accs[a, c], axis=0, keepdims=True) for a in range(first, first + half) for c in range(vectors)]
    return jnp.concatenate(sums, axis=0)


def tile_of(ref, v, block, lane):
    return ref[v, block * TILE : (block + 1) * TILE, lane : lane + 128]


def own_kernel(drift_ref, k_ref, beyond_ref, table_ref, shifted_ref):
    vectors, rows, cols = k_ref.shape
    tile = functools.partial(tile_of, k_ref)
    table_ref[...] = pair_sums(tile, tile, rows // TILE, vectors, cols)
    total = rows + beyond_ref.shape[1]
    by = lax.rem(total - drift_ref[0], total)
    for b in range(vectors):
        joined = jnp.concatenate([k_ref[b], beyond_ref[b]], axis=0)
        shifted_ref[b] = pltpu.roll(joined, by, 0)[:rows]


def gram_kernel(shifted_ref, mid_ref, edge_ref, own_ref, gram_ref):
    vectors, rows, cols = shifted_ref.shape
    blocks = rows // TILE

    def arrived(c, block, lane):
        if block == 0:
            return tile_of(edge_ref, c, 1, lane)
        if block == blocks - 1:
            return tile_of(edge_ref, c, 0, lane)
        return tile_of(mid_ref, c, block - 1, lane)

    table = own_ref[...] - pair_sums(functools.partial(tile_of, shifted_ref), arrived, blocks, vectors, cols)
    ones = jnp.ones((gram_ref.shape[0], 128), jnp.float32)
    gram_ref[...] = lax.dot_general(
        ones, table, (((1,), (1,)), ((), ())),
        precision=lax.Precision.HIGHEST, preferred_element_type=jnp.float32,
    )


def last_kernel(drift_ref, k_ref, mid_ref, edge_ref, rim_mid_ref, rim_hi_ref, product_ref):
    vectors, rows, _ = k_ref.shape
    total = DRIFT + rows
    by = lax.rem(drift_ref[0] + (total - DRIFT), total)
    for b in range(vectors):
        joined = jnp.concatenate(
            [rim_mid_ref[b], rim_hi_ref[b], edge_ref[b, TILE:], mid_ref[b], edge_ref[b, :TILE]], axis=0
        )
        product_ref[b] = k_ref[b] - pltpu.roll(joined, by, 0)[:rows]


def buffer(*shape):
    return pltpu.VMEM(shape, jnp.float32)


def call(kernel, outs, ins, scratch, cost, limit=LIMIT):
    return pl.pallas_call(
        kernel,
        out_shape=[jax.ShapeDtypeStruct(o, jnp.float32) for o in outs],
        in_specs=ins,
        out_specs=[VMEM] * len(outs),
        scratch_shapes=scratch,
        compiler_params=pltpu.CompilerParams(vmem_limit_bytes=limit),
        cost_estimate=pl.CostEstimate(flops=cost << 30, bytes_accessed=4 << 20, transcendentals=0),
    )


def body(krylov, advect_x, advect_y, step_counts, drifts):
    k, ax, ay = krylov[0], advect_x[0], advect_y[0]
    vectors, rows, cols = k.shape
    segs, strips = lax.axis_size("seg"), lax.axis_size("gx")
    world, pairs = segs * strips, vectors * vectors
    half = segs // 2
    onward = functools.partial(lax.ppermute, axis_name="seg", perm=shift_pairs(segs, 1))
    sideways = functools.partial(lax.ppermute, axis_name="gx", perm=shift_pairs(strips, 1))
    backward = functools.partial(lax.ppermute, axis_name="gx", perm=shift_pairs(strips, -1))

    fields = vectors + 2
    head, tail = call(
        pack_kernel,
        [(fields, STEPS, cols)] * 2,
        [ANY] * 3,
        [buffer(fields, TILE, cols), buffer(fields, TILE, cols), pltpu.SemaphoreType.DMA((2, 3))],
        1,
        limit=FULL,
    )(k, ax, ay)
    right = backward(head)
    left = sideways(tail)
    drift = onward(drifts)
    mid, beyond = call(
        inner_kernel,
        [(vectors, rows - 2 * TILE, cols), (vectors, DRIFT, cols)],
        [SMEM, VMEM, VMEM, VMEM],
        [buffer(vectors, rows, cols), buffer(4, rows, cols)],
        64,
    )(step_counts, k, ax, ay)
    beyond, right, left = lax.optimization_barrier((beyond, right, left))
    beyond = backward(beyond)
    mid = lax.ppermute(mid, "seg", [(s, s // half * half + (s + 1) % half) for s in range(segs)])
    (edge,) = call(
        outer_kernel,
        [(vectors, 2 * TILE, cols)],
        [SMEM] + [VMEM] * 5,
        [buffer(vectors, 5 * TILE, cols), buffer(4, 5 * TILE, cols)],
        1,
    )(step_counts, k, ax, ay, left, right)
    sent, kept = lax.optimization_barrier((edge, k))
    edge = onward(edge)
    own, shifted = call(own_kernel, [(pairs, 128), k.shape], [SMEM, VMEM, VMEM], [], 16)(drift, kept, beyond)
    held, _ = lax.optimization_barrier((mid, sent))
    crossed = lax.ppermute(held, "seg", [(0, half), (half, 0)])
    mid = jnp.where(lax.axis_index("seg") % half == 0, crossed, mid)
    rim_mid = sideways(mid[:, -(DRIFT - TILE) :])
    edge, own, _ = lax.optimization_barrier((edge, own, mid))
    rim_hi = sideways(edge[:, :TILE])
    (gram,) = call(gram_kernel, [(world, pairs)], [VMEM] * 4, [], 1)(shifted, mid, edge, own)
    gram = lax.all_to_all(gram, ("seg", "gx"), 0, 0)
    (product,) = call(last_kernel, [k.shape], [SMEM] + [VMEM] * 5, [], 1)(
        drift, k, mid, edge, rim_mid, rim_hi
    )
    product, gram = lax.optimization_barrier((product, gram))
    cells = world * rows * cols
    gram = jnp.sum(gram, axis=0).reshape(vectors, vectors) / jnp.float32(cells)
    return product[None], gram


def solution(mesh):
    return jax.shard_map(
        body,
        mesh=mesh,
        in_specs=(
            P("seg", None, "gx", None),
            P("seg", "gx", None),
            P("seg", "gx", None),
            P("seg"),
            P("seg"),
        ),
        out_specs=(P("seg", None, "gx", None), P()),
        check_vma=False,
    )
```

```python
import functools
import jax
import jax.numpy as jnp
from jax import lax
from jax.experimental import pallas as pl
from jax.experimental.pallas import tpu as pltpu
from jax.sharding import PartitionSpec as P

STEPS = 4
DRIFT = 16
TILE = 8

ANY = pl.BlockSpec(memory_space=pl.ANY)
VMEM = pl.BlockSpec(memory_space=pltpu.VMEM)
SMEM = pl.BlockSpec(memory_space=pltpu.SMEM)
LIMIT = 12 * 1024 * 1024
FULL = 60 * 1024 * 1024


def shift_pairs(count, by):
    return [(i, (i + by) % count) for i in range(count)]


def weights(ax, ay):
    col = lax.broadcasted_iota(jnp.int32, ax.shape, 1)
    last = ax.shape[1] - 1
    return (
        0.2 - ax,
        0.2 + ax,
        jnp.where(col == last, 0.0, 0.2 - ay),
        jnp.where(col == 0, 0.0, 0.2 + ay),
    )


def step(q, we, ww, wn, ws):
    rows, cols = q.shape
    return (
        0.2 * q
        + we * pltpu.roll(q, rows - 1, 0)
        + ww * pltpu.roll(q, 1, 0)
        + wn * pltpu.roll(q, cols - 1, 1)
        + ws * pltpu.roll(q, 1, 1)
    )


def pack_kernel(k_any, ax_any, ay_any, head_ref, tail_ref, low_ref, high_ref, sems):
    rows = k_any.shape[1]
    vectors = k_any.shape[0]
    copies = []
    for i, (at, target) in enumerate(((0, low_ref), (rows - TILE, high_ref))):
        copies += [
            pltpu.make_async_copy(k_any.at[:, pl.ds(at, TILE)], target.at[pl.ds(0, vectors)], sems.at[i, 0]),
            pltpu.make_async_copy(ax_any.at[pl.ds(at, TILE)], target.at[vectors], sems.at[i, 1]),
            pltpu.make_async_copy(ay_any.at[pl.ds(at, TILE)], target.at[vectors + 1], sems.at[i, 2]),
        ]
    for copy in copies:
        copy.start()
    for copy in copies:
        copy.wait()
    head_ref[...] = low_ref[:, :STEPS]
    tail_ref[...] = high_ref[:, TILE - STEPS :]


def inner_kernel(count_ref, k_ref, ax_ref, ay_ref, mid_ref, beyond_ref, q_ref, w_ref):
    vectors, rows, _ = k_ref.shape
    for i, w in enumerate(weights(ax_ref[...], ay_ref[...])):
        w_ref[i] = w
    q_ref[...] = k_ref[...]
    beyond_ref[...] = k_ref[:, :DRIFT]

    @pl.loop(0, count_ref[0])
    def _(_):
        for b in range(vectors):
            q_ref[b] = step(q_ref[b], w_ref[0], w_ref[1], w_ref[2], w_ref[3])

    mid_ref[...] = q_ref[:, TILE : rows - TILE]


def outer_kernel(count_ref, k_ref, ax_ref, ay_ref, left_ref, right_ref, out_ref, q_ref, w_ref):
    vectors, rows, _ = k_ref.shape

    def around(strip, at):
        return jnp.concatenate(
            [strip[rows - 2 * TILE :], right_ref[at], left_ref[at], strip[: 2 * TILE]], axis=0
        )

    for i, w in enumerate(weights(around(ax_ref, vectors), around(ay_ref, vectors + 1))):
        w_ref[i] = w
    for b in range(vectors):
        q_ref[b] = around(k_ref.at[b], b)

    @pl.loop(0, count_ref[0])
    def _(_):
        for b in range(vectors):
            q_ref[b] = step(q_ref[b], w_ref[0], w_ref[1], w_ref[2], w_ref[3])

    out_ref[:, :TILE] = q_ref[:, TILE : 2 * TILE]
    out_ref[:, TILE:] = q_ref[:, 3 * TILE : 4 * TILE]


def pair_sums(left, right, blocks, vectors, cols):
    sums = []
    half = vectors // 2
    for first in range(0, vectors, half):
        accs = {}
        for block in range(blocks):
            for lane in range(0, cols, 128):
                rs = [right(c, block, lane) for c in range(vectors)]
                for a in range(first, first + half):
                    value = left(a, block, lane)
                    for c in range(vectors):
                        term = value * rs[c]
                        accs[a, c] = accs[a, c] + term if (a, c) in accs else term
        sums += [jnp.sum(accs[a, c], axis=0, keepdims=True) for a in range(first, first + half) for c in range(vectors)]
    return jnp.concatenate(sums, axis=0)


def tile_of(ref, v, block, lane):
    return ref[v, block * TILE : (block + 1) * TILE, lane : lane + 128]


def own_kernel(drift_ref, k_ref, beyond_ref, table_ref, shifted_ref):
    vectors, rows, cols = k_ref.shape
    tile = functools.partial(tile_of, k_ref)
    table_ref[...] = pair_sums(tile, tile, rows // TILE, vectors, cols)
    total = rows + beyond_ref.shape[1]
    by = lax.rem(total - drift_ref[0], total)
    for b in range(vectors):
        joined = jnp.concatenate([k_ref[b], beyond_ref[b]], axis=0)
        shifted_ref[b] = pltpu.roll(joined, by, 0)[:rows]


def gram_kernel(
    drift_ref, k_ref, shifted_ref, mid_ref, edge_ref, upper_ref, own_ref, gram_ref, before_ref
):
    vectors, rows, cols = k_ref.shape
    drift = drift_ref[0]
    blocks = rows // TILE
    row = lax.broadcasted_iota(jnp.int32, (DRIFT, cols), 0)
    for b in range(vectors):
        before_ref[b] = jnp.where(row < drift, pltpu.roll(upper_ref[b], lax.rem(drift, DRIFT), 0), 0.0)

    def left(a, block, lane):
        if block < blocks:
            return tile_of(shifted_ref, a, block, lane)
        return tile_of(k_ref, a, block - blocks, lane)

    def right(c, block, lane):
        if block == 0:
            return tile_of(edge_ref, c, 1, lane)
        if block < blocks - 1:
            return tile_of(mid_ref, c, block - 1, lane)
        if block == blocks - 1:
            return tile_of(edge_ref, c, 0, lane)
        return tile_of(before_ref, c, block - blocks, lane)

    table = own_ref[...] - pair_sums(left, right, blocks + DRIFT // TILE, vectors, cols)
    ones = jnp.ones((gram_ref.shape[0], 128), jnp.float32)
    gram_ref[...] = lax.dot_general(
        ones, table, (((1,), (1,)), ((), ())),
        precision=lax.Precision.HIGHEST, preferred_element_type=jnp.float32,
    )


def last_kernel(drift_ref, k_ref, mid_ref, edge_ref, rim_mid_ref, rim_hi_ref, upper_ref, product_ref):
    vectors, rows, _ = k_ref.shape
    total = DRIFT + rows
    by = lax.rem(drift_ref[0] + (total - DRIFT), total)
    for b in range(vectors):
        joined = jnp.concatenate(
            [rim_mid_ref[b] + upper_ref[b, :TILE], rim_hi_ref[b] + upper_ref[b, TILE:], edge_ref[b, TILE:], mid_ref[b], edge_ref[b, :TILE]], axis=0
        )
        product_ref[b] = k_ref[b] - pltpu.roll(joined, by, 0)[:rows]


def buffer(*shape):
    return pltpu.VMEM(shape, jnp.float32)


def call(kernel, outs, ins, scratch, cost, limit=LIMIT):
    return pl.pallas_call(
        kernel,
        out_shape=[jax.ShapeDtypeStruct(o, jnp.float32) for o in outs],
        in_specs=ins,
        out_specs=[VMEM] * len(outs),
        scratch_shapes=scratch,
        compiler_params=pltpu.CompilerParams(vmem_limit_bytes=limit),
        cost_estimate=pl.CostEstimate(flops=cost << 30, bytes_accessed=4 << 20, transcendentals=0),
    )


def rim_pairs(segs, strips, direct):
    pairs = []
    for s in range(segs):
        for g in range(strips):
            busy = (s + 1) % (segs // 2) == 0 and g % 2 == 1
            if busy == direct:
                pairs.append(((s - direct) * strips + g, s * strips + (g + 1) % strips))
    return pairs


def body(krylov, advect_x, advect_y, step_counts, drifts):
    k, ax, ay = krylov[0], advect_x[0], advect_y[0]
    vectors, rows, cols = k.shape
    segs, strips = lax.axis_size("seg"), lax.axis_size("gx")
    world, pairs = segs * strips, vectors * vectors
    onward = functools.partial(lax.ppermute, axis_name="seg", perm=shift_pairs(segs, 1))
    along = rim_pairs(segs, strips, False)
    sideways = functools.partial(lax.ppermute, axis_name=("seg", "gx"), perm=along)
    backward = functools.partial(lax.ppermute, axis_name=("seg", "gx"), perm=[(b, a) for a, b in along])
    ahead = functools.partial(lax.ppermute, axis_name=("seg", "gx"), perm=rim_pairs(segs, strips, True))

    fields = vectors + 2
    head, tail = call(
        pack_kernel,
        [(fields, STEPS, cols)] * 2,
        [ANY] * 3,
        [buffer(fields, TILE, cols), buffer(fields, TILE, cols), pltpu.SemaphoreType.DMA((2, 3))],
        1,
        limit=FULL,
    )(k, ax, ay)
    right = lax.ppermute(head, "gx", shift_pairs(strips, -1))
    left = lax.ppermute(tail, "gx", shift_pairs(strips, 1))
    drift = onward(drifts)
    mid, beyond = call(
        inner_kernel,
        [(vectors, rows - 2 * TILE, cols), (vectors, DRIFT, cols)],
        [SMEM, VMEM, VMEM, VMEM],
        [buffer(vectors, rows, cols), buffer(4, rows, cols)],
        64,
    )(step_counts, k, ax, ay)
    beyond, right, left = lax.optimization_barrier((beyond, right, left))
    beyond = backward(beyond)
    inner = mid[:, -(DRIFT - TILE) :]
    mid = onward(mid)
    (edge,) = call(
        outer_kernel,
        [(vectors, 2 * TILE, cols)],
        [SMEM] + [VMEM] * 5,
        [buffer(vectors, 5 * TILE, cols), buffer(4, 5 * TILE, cols)],
        1,
    )(step_counts, k, ax, ay, left, right)
    kept, outer = lax.optimization_barrier((k, edge))
    edge = onward(edge)
    upper = ahead(jnp.concatenate([inner, outer[:, :TILE]], axis=1))
    own, shifted = call(own_kernel, [(pairs, 128), k.shape], [SMEM, VMEM, VMEM], [], 16)(drift, kept, beyond)
    rim_mid = sideways(mid[:, -(DRIFT - TILE) :])
    edge, own, _ = lax.optimization_barrier((edge, own, mid))
    rim_hi = sideways(edge[:, :TILE])
    (gram,) = call(
        gram_kernel, [(world, pairs)], [SMEM] + [VMEM] * 6, [buffer(vectors, DRIFT, cols)], 1
    )(drift, k, shifted, mid, edge, upper, own)
    gram = lax.all_to_all(gram, ("seg", "gx"), 0, 0)
    (product,) = call(last_kernel, [k.shape], [SMEM] + [VMEM] * 6, [], 1)(
        drift, k, mid, edge, rim_mid, rim_hi, upper
    )
    product, gram = lax.optimization_barrier((product, gram))
    cells = world * rows * cols
    gram = jnp.sum(gram, axis=0).reshape(vectors, vectors) / jnp.float32(cells)
    return product[None], gram


def solution(mesh):
    return jax.shard_map(
        body,
        mesh=mesh,
        in_specs=(
            P("seg", None, "gx", None),
            P("seg", "gx", None),
            P("seg", "gx", None),
            P("seg"),
            P("seg"),
        ),
        out_specs=(P("seg", None, "gx", None), P()),
        check_vma=False,
    )
```

```python
import functools
import jax
import jax.numpy as jnp
from jax import lax
from jax.experimental import pallas as pl
from jax.experimental.pallas import tpu as pltpu
from jax.sharding import PartitionSpec as P

STEPS = 4
DRIFT = 16
TILE = 8

ANY = pl.BlockSpec(memory_space=pl.ANY)
VMEM = pl.BlockSpec(memory_space=pltpu.VMEM)
SMEM = pl.BlockSpec(memory_space=pltpu.SMEM)
LIMIT = 12 * 1024 * 1024
FULL = 60 * 1024 * 1024


def shift_pairs(count, by):
    return [(i, (i + by) % count) for i in range(count)]


def weights(ax, ay):
    col = lax.broadcasted_iota(jnp.int32, ax.shape, 1)
    last = ax.shape[1] - 1
    return (
        0.2 - ax,
        0.2 + ax,
        jnp.where(col == last, 0.0, 0.2 - ay),
        jnp.where(col == 0, 0.0, 0.2 + ay),
    )


def step(q, we, ww, wn, ws):
    rows, cols = q.shape
    return (
        0.2 * q
        + we * pltpu.roll(q, rows - 1, 0)
        + ww * pltpu.roll(q, 1, 0)
        + wn * pltpu.roll(q, cols - 1, 1)
        + ws * pltpu.roll(q, 1, 1)
    )


def pack_kernel(k_any, ax_any, ay_any, head_ref, tail_ref, low_ref, high_ref, sems):
    rows = k_any.shape[1]
    vectors = k_any.shape[0]
    copies = []
    for i, (at, target) in enumerate(((0, low_ref), (rows - TILE, high_ref))):
        copies += [
            pltpu.make_async_copy(k_any.at[:, pl.ds(at, TILE)], target.at[pl.ds(0, vectors)], sems.at[i, 0]),
            pltpu.make_async_copy(ax_any.at[pl.ds(at, TILE)], target.at[vectors], sems.at[i, 1]),
            pltpu.make_async_copy(ay_any.at[pl.ds(at, TILE)], target.at[vectors + 1], sems.at[i, 2]),
        ]
    for copy in copies:
        copy.start()
    for copy in copies:
        copy.wait()
    head_ref[...] = low_ref[:, :STEPS]
    tail_ref[...] = high_ref[:, TILE - STEPS :]


def inner_kernel(count_ref, k_ref, ax_ref, ay_ref, mid_ref, beyond_ref, q_ref, w_ref):
    vectors, rows, _ = k_ref.shape
    for i, w in enumerate(weights(ax_ref[...], ay_ref[...])):
        w_ref[i] = w
    q_ref[...] = k_ref[...]

    @pl.loop(0, count_ref[0])
    def _(_):
        for b in range(vectors):
            q_ref[b] = step(q_ref[b], w_ref[0], w_ref[1], w_ref[2], w_ref[3])

    mid_ref[...] = q_ref[:, TILE : rows - TILE]
    beyond_ref[...] = k_ref[:, :DRIFT]


def outer_kernel(count_ref, k_ref, ax_ref, ay_ref, left_ref, right_ref, edge_ref, table_ref, q_ref, w_ref):
    vectors, rows, _ = k_ref.shape

    def around(strip, at):
        return jnp.concatenate(
            [strip[rows - 2 * TILE :], right_ref[at], left_ref[at], strip[: 2 * TILE]], axis=0
        )

    for i, w in enumerate(weights(around(ax_ref, vectors), around(ay_ref, vectors + 1))):
        w_ref[i] = w
    for b in range(vectors):
        q_ref[b] = around(k_ref.at[b], b)

    @pl.loop(0, count_ref[0])
    def _(_):
        for b in range(vectors):
            q_ref[b] = step(q_ref[b], w_ref[0], w_ref[1], w_ref[2], w_ref[3])

    edge_ref[:, :TILE] = q_ref[:, TILE : 2 * TILE]
    edge_ref[:, TILE:] = q_ref[:, 3 * TILE : 4 * TILE]
    tile = functools.partial(tile_of, k_ref)
    table_ref[...] = pair_sums(tile, tile, rows // TILE, vectors, k_ref.shape[2])


def pair_sums(left, right, blocks, vectors, cols):
    sums = []
    half = vectors // 2
    for first in range(0, vectors, half):
        accs = {}
        for block in range(blocks):
            for lane in range(0, cols, 128):
                rs = [right(c, block, lane) for c in range(vectors)]
                for a in range(first, first + half):
                    value = left(a, block, lane)
                    for c in range(vectors):
                        term = value * rs[c]
                        accs[a, c] = accs[a, c] + term if (a, c) in accs else term
        sums += [jnp.sum(accs[a, c], axis=0, keepdims=True) for a in range(first, first + half) for c in range(vectors)]
    return jnp.concatenate(sums, axis=0)


def tile_of(ref, v, block, lane):
    return ref[v, block * TILE : (block + 1) * TILE, lane : lane + 128]


def gram_kernel(
    drift_ref, k_ref, beyond_ref, mid_ref, edge_ref, upper_ref, own_ref, gram_ref, near_ref, shifted_ref, before_ref
):
    vectors, rows, cols = k_ref.shape
    drift = drift_ref[0]
    blocks = rows // TILE
    near_ref[:, : DRIFT - TILE] = mid_ref[:, -(DRIFT - TILE) :]
    near_ref[:, DRIFT - TILE :] = edge_ref[:, :TILE]
    total = rows + DRIFT
    back = lax.rem(total - drift, total)
    row = lax.broadcasted_iota(jnp.int32, (DRIFT, cols), 0)
    for b in range(vectors):
        joined = jnp.concatenate([k_ref[b], beyond_ref[b]], axis=0)
        shifted_ref[b] = pltpu.roll(joined, back, 0)[:rows]
        before_ref[b] = jnp.where(row < drift, pltpu.roll(upper_ref[b], lax.rem(drift, DRIFT), 0), 0.0)

    def left(a, block, lane):
        if block < blocks:
            return tile_of(shifted_ref, a, block, lane)
        return tile_of(k_ref, a, block - blocks, lane)

    def right(c, block, lane):
        if block == 0:
            return tile_of(edge_ref, c, 1, lane)
        if block < blocks - 1:
            return tile_of(mid_ref, c, block - 1, lane)
        if block == blocks - 1:
            return tile_of(edge_ref, c, 0, lane)
        return tile_of(before_ref, c, block - blocks, lane)

    table = own_ref[...] - pair_sums(left, right, blocks + DRIFT // TILE, vectors, cols)
    ones = jnp.ones((gram_ref.shape[0], 128), jnp.float32)
    gram_ref[...] = lax.dot_general(
        ones, table, (((1,), (1,)), ((), ())),
        precision=lax.Precision.HIGHEST, preferred_element_type=jnp.float32,
    )


def last_kernel(drift_ref, k_ref, mid_ref, edge_ref, rim_ref, upper_ref, product_ref):
    vectors, rows, _ = k_ref.shape
    total = DRIFT + rows
    by = lax.rem(drift_ref[0] + (total - DRIFT), total)
    for b in range(vectors):
        joined = jnp.concatenate(
            [rim_ref[b] + upper_ref[b], edge_ref[b, TILE:], mid_ref[b], edge_ref[b, :TILE]], axis=0
        )
        product_ref[b] = k_ref[b] - pltpu.roll(joined, by, 0)[:rows]


def buffer(*shape):
    return pltpu.VMEM(shape, jnp.float32)


def call(kernel, outs, ins, scratch, cost, limit=LIMIT):
    return pl.pallas_call(
        kernel,
        out_shape=[jax.ShapeDtypeStruct(o, jnp.float32) for o in outs],
        in_specs=ins,
        out_specs=[VMEM] * len(outs),
        scratch_shapes=scratch,
        compiler_params=pltpu.CompilerParams(vmem_limit_bytes=limit),
        cost_estimate=pl.CostEstimate(flops=cost << 30, bytes_accessed=cost << 20, transcendentals=0),
    )


def rim_pairs(segs, strips, direct):
    pairs = []
    for s in range(segs):
        for g in range(strips):
            crosses = g % 2 == 1 and s % (segs // 2) != 0
            if crosses == direct:
                pairs.append((((s - direct) % segs) * strips + g, s * strips + (g + 1) % strips))
    return pairs


def body(krylov, advect_x, advect_y, step_counts, drifts):
    k, ax, ay = krylov[0], advect_x[0], advect_y[0]
    vectors, rows, cols = k.shape
    segs, strips = lax.axis_size("seg"), lax.axis_size("gx")
    world, pairs = segs * strips, vectors * vectors
    fields = vectors + 2
    onward = functools.partial(lax.ppermute, axis_name="seg", perm=shift_pairs(segs, 1))
    along = rim_pairs(segs, strips, False)
    sideways = functools.partial(lax.ppermute, axis_name=("seg", "gx"), perm=along)
    backward = functools.partial(lax.ppermute, axis_name=("seg", "gx"), perm=[(b, a) for a, b in along])
    ahead = functools.partial(lax.ppermute, axis_name=("seg", "gx"), perm=rim_pairs(segs, strips, True))

    head, tail = call(
        pack_kernel,
        [(fields, STEPS, cols)] * 2,
        [ANY] * 3,
        [buffer(fields, TILE, cols), buffer(fields, TILE, cols), pltpu.SemaphoreType.DMA((2, 3))],
        1,
        limit=FULL,
    )(k, ax, ay)
    right = lax.ppermute(head, "gx", shift_pairs(strips, -1))
    left = lax.ppermute(tail, "gx", shift_pairs(strips, 1))
    mid, beyond = call(
        inner_kernel,
        [(vectors, rows - 2 * TILE, cols), (vectors, DRIFT, cols)],
        [SMEM, VMEM, VMEM, VMEM],
        [buffer(vectors, rows, cols), buffer(4, rows, cols)],
        64,
    )(step_counts, k, ax, ay)
    drift = onward(drifts)
    edge, own = call(
        outer_kernel,
        [(vectors, 2 * TILE, cols), (pairs, 128)],
        [SMEM] + [VMEM] * 5,
        [buffer(vectors, 5 * TILE, cols), buffer(4, 5 * TILE, cols)],
        0,
    )(step_counts, k, ax, ay, left, right)
    upper = ahead(jnp.concatenate([mid[:, -(DRIFT - TILE) :], edge[:, :TILE]], axis=1))
    beyond, _ = lax.optimization_barrier((beyond, edge))
    beyond = backward(beyond)
    mid = onward(mid)
    edge = onward(edge)
    gram, near = call(
        gram_kernel,
        [(world, pairs), (vectors, DRIFT, cols)],
        [SMEM] + [VMEM] * 6,
        [buffer(*k.shape), buffer(vectors, DRIFT, cols)],
        1,
    )(drift, k, beyond, mid, edge, upper, own)
    rim = sideways(near)
    gram = lax.all_to_all(gram, ("seg", "gx"), 0, 0)
    (product,) = call(last_kernel, [k.shape], [SMEM] + [VMEM] * 5, [], 1)(
        drift, k, mid, edge, rim, upper
    )
    product, gram = lax.optimization_barrier((product, gram))
    cells = world * rows * cols
    gram = jnp.sum(gram, axis=0).reshape(vectors, vectors) / jnp.float32(cells)
    return product[None], gram


def solution(mesh):
    return jax.shard_map(
        body,
        mesh=mesh,
        in_specs=(
            P("seg", None, "gx", None),
            P("seg", "gx", None),
            P("seg", "gx", None),
            P("seg"),
            P("seg"),
        ),
        out_specs=(P("seg", None, "gx", None), P()),
        check_vma=False,
    )
```

```python
import functools
import jax
import jax.numpy as jnp
from jax import lax
from jax.experimental import pallas as pl
from jax.experimental.pallas import tpu as pltpu
from jax.sharding import PartitionSpec as P

STEPS = 4
DRIFT = 16
TILE = 8

ANY = pl.BlockSpec(memory_space=pl.ANY)
VMEM = pl.BlockSpec(memory_space=pltpu.VMEM)
SMEM = pl.BlockSpec(memory_space=pltpu.SMEM)
LIMIT = 12 * 1024 * 1024
FULL = 60 * 1024 * 1024


def shift_pairs(count, by):
    return [(i, (i + by) % count) for i in range(count)]


def weights(ax, ay):
    col = lax.broadcasted_iota(jnp.int32, ax.shape, 1)
    last = ax.shape[1] - 1
    return (
        0.2 - ax,
        0.2 + ax,
        jnp.where(col == last, 0.0, 0.2 - ay),
        jnp.where(col == 0, 0.0, 0.2 + ay),
    )


def step(q, we, ww, wn, ws):
    rows, cols = q.shape
    return (
        0.2 * q
        + we * pltpu.roll(q, rows - 1, 0)
        + ww * pltpu.roll(q, 1, 0)
        + wn * pltpu.roll(q, cols - 1, 1)
        + ws * pltpu.roll(q, 1, 1)
    )


def pack_kernel(k_any, ax_any, ay_any, head_ref, tail_ref, low_ref, high_ref, sems):
    rows = k_any.shape[1]
    vectors = k_any.shape[0]
    copies = []
    for i, (at, target) in enumerate(((0, low_ref), (rows - TILE, high_ref))):
        copies += [
            pltpu.make_async_copy(k_any.at[:, pl.ds(at, TILE)], target.at[pl.ds(0, vectors)], sems.at[i, 0]),
            pltpu.make_async_copy(ax_any.at[pl.ds(at, TILE)], target.at[vectors], sems.at[i, 1]),
            pltpu.make_async_copy(ay_any.at[pl.ds(at, TILE)], target.at[vectors + 1], sems.at[i, 2]),
        ]
    for copy in copies:
        copy.start()
    for copy in copies:
        copy.wait()
    head_ref[...] = low_ref[:, :STEPS]
    tail_ref[...] = high_ref[:, TILE - STEPS :]


def inner_kernel(count_ref, k_ref, ax_ref, ay_ref, mid_ref, beyond_ref, q_ref, w_ref):
    vectors, rows, _ = k_ref.shape
    for i, w in enumerate(weights(ax_ref[...], ay_ref[...])):
        w_ref[i] = w
    q_ref[...] = k_ref[...]
    beyond_ref[...] = k_ref[:, :DRIFT]

    @pl.loop(0, count_ref[0])
    def _(_):
        for b in range(vectors):
            q_ref[b] = step(q_ref[b], w_ref[0], w_ref[1], w_ref[2], w_ref[3])

    mid_ref[...] = q_ref[:, TILE : rows - TILE]


def outer_kernel(count_ref, k_ref, ax_ref, ay_ref, left_ref, right_ref, out_ref, q_ref, w_ref):
    vectors, rows, _ = k_ref.shape

    def around(strip, at):
        return jnp.concatenate(
            [strip[rows - 2 * TILE :], right_ref[at], left_ref[at], strip[: 2 * TILE]], axis=0
        )

    for i, w in enumerate(weights(around(ax_ref, vectors), around(ay_ref, vectors + 1))):
        w_ref[i] = w
    for b in range(vectors):
        q_ref[b] = around(k_ref.at[b], b)

    @pl.loop(0, count_ref[0])
    def _(_):
        for b in range(vectors):
            q_ref[b] = step(q_ref[b], w_ref[0], w_ref[1], w_ref[2], w_ref[3])

    out_ref[:, :TILE] = q_ref[:, TILE : 2 * TILE]
    out_ref[:, TILE:] = q_ref[:, 3 * TILE : 4 * TILE]


def pair_sums(left, right, blocks, vectors, cols):
    sums = []
    half = vectors // 2
    for first in range(0, vectors, half):
        accs = {}
        for block in range(blocks):
            for lane in range(0, cols, 128):
                rs = [right(c, block, lane) for c in range(vectors)]
                for a in range(first, first + half):
                    value = left(a, block, lane)
                    for c in range(vectors):
                        term = value * rs[c]
                        accs[a, c] = accs[a, c] + term if (a, c) in accs else term
        sums += [jnp.sum(accs[a, c], axis=0, keepdims=True) for a in range(first, first + half) for c in range(vectors)]
    return jnp.concatenate(sums, axis=0)


def tile_of(ref, v, block, lane):
    return ref[v, block * TILE : (block + 1) * TILE, lane : lane + 128]


def own_kernel(drift_ref, k_ref, beyond_ref, table_ref, shifted_ref):
    vectors, rows, cols = k_ref.shape
    tile = functools.partial(tile_of, k_ref)
    table_ref[...] = pair_sums(tile, tile, rows // TILE, vectors, cols)
    total = rows + beyond_ref.shape[1]
    by = lax.rem(total - drift_ref[0], total)
    for b in range(vectors):
        joined = jnp.concatenate([k_ref[b], beyond_ref[b]], axis=0)
        shifted_ref[b] = pltpu.roll(joined, by, 0)[:rows]


def gram_kernel(
    drift_ref, k_ref, shifted_ref, mid_ref, edge_ref, upper_ref, own_ref, gram_ref, before_ref
):
    vectors, rows, cols = k_ref.shape
    drift = drift_ref[0]
    blocks = rows // TILE
    row = lax.broadcasted_iota(jnp.int32, (DRIFT, cols), 0)
    for b in range(vectors):
        before_ref[b] = jnp.where(row < drift, pltpu.roll(upper_ref[b], lax.rem(drift, DRIFT), 0), 0.0)

    def left(a, block, lane):
        if block < blocks:
            return tile_of(shifted_ref, a, block, lane)
        return tile_of(k_ref, a, block - blocks, lane)

    def right(c, block, lane):
        if block == 0:
            return tile_of(edge_ref, c, 1, lane)
        if block < blocks - 1:
            return tile_of(mid_ref, c, block - 1, lane)
        if block == blocks - 1:
            return tile_of(edge_ref, c, 0, lane)
        return tile_of(before_ref, c, block - blocks, lane)

    table = own_ref[...] - pair_sums(left, right, blocks + DRIFT // TILE, vectors, cols)
    ones = jnp.ones((gram_ref.shape[0], 128), jnp.float32)
    gram_ref[...] = lax.dot_general(
        ones, table, (((1,), (1,)), ((), ())),
        precision=lax.Precision.HIGHEST, preferred_element_type=jnp.float32,
    )


def last_kernel(drift_ref, k_ref, mid_ref, edge_ref, rim_mid_ref, rim_hi_ref, upper_ref, product_ref):
    vectors, rows, _ = k_ref.shape
    total = DRIFT + rows
    by = lax.rem(drift_ref[0] + (total - DRIFT), total)
    for b in range(vectors):
        joined = jnp.concatenate(
            [rim_mid_ref[b] + upper_ref[b, :TILE], rim_hi_ref[b] + upper_ref[b, TILE:], edge_ref[b, TILE:], mid_ref[b], edge_ref[b, :TILE]], axis=0
        )
        product_ref[b] = k_ref[b] - pltpu.roll(joined, by, 0)[:rows]


def buffer(*shape):
    return pltpu.VMEM(shape, jnp.float32)


def call(kernel, outs, ins, scratch, cost, limit=LIMIT):
    return pl.pallas_call(
        kernel,
        out_shape=[jax.ShapeDtypeStruct(o, jnp.float32) for o in outs],
        in_specs=ins,
        out_specs=[VMEM] * len(outs),
        scratch_shapes=scratch,
        compiler_params=pltpu.CompilerParams(vmem_limit_bytes=limit),
        cost_estimate=pl.CostEstimate(flops=cost << 30, bytes_accessed=4 << 20, transcendentals=0),
    )


def rim_pairs(segs, strips, direct):
    pairs = []
    for s in range(segs):
        for g in range(strips):
            crosses = g % 2 == 1 and s % (segs // 2) != 0
            if crosses == direct:
                pairs.append((((s - direct) % segs) * strips + g, s * strips + (g + 1) % strips))
    return pairs


def body(krylov, advect_x, advect_y, step_counts, drifts):
    k, ax, ay = krylov[0], advect_x[0], advect_y[0]
    vectors, rows, cols = k.shape
    segs, strips = lax.axis_size("seg"), lax.axis_size("gx")
    world, pairs = segs * strips, vectors * vectors
    onward = functools.partial(lax.ppermute, axis_name="seg", perm=shift_pairs(segs, 1))
    along = rim_pairs(segs, strips, False)
    sideways = functools.partial(lax.ppermute, axis_name=("seg", "gx"), perm=along)
    backward = functools.partial(lax.ppermute, axis_name=("seg", "gx"), perm=[(b, a) for a, b in along])
    ahead = functools.partial(lax.ppermute, axis_name=("seg", "gx"), perm=rim_pairs(segs, strips, True))

    fields = vectors + 2
    head, tail = call(
        pack_kernel,
        [(fields, STEPS, cols)] * 2,
        [ANY] * 3,
        [buffer(fields, TILE, cols), buffer(fields, TILE, cols), pltpu.SemaphoreType.DMA((2, 3))],
        1,
        limit=FULL,
    )(k, ax, ay)
    right = lax.ppermute(head, "gx", shift_pairs(strips, -1))
    left = lax.ppermute(tail, "gx", shift_pairs(strips, 1))
    drift = onward(drifts)
    mid, beyond = call(
        inner_kernel,
        [(vectors, rows - 2 * TILE, cols), (vectors, DRIFT, cols)],
        [SMEM, VMEM, VMEM, VMEM],
        [buffer(vectors, rows, cols), buffer(4, rows, cols)],
        64,
    )(step_counts, k, ax, ay)
    beyond, right, left = lax.optimization_barrier((beyond, right, left))
    beyond = backward(beyond)
    inner = mid[:, -(DRIFT - TILE) :]
    mid = onward(mid)
    (edge,) = call(
        outer_kernel,
        [(vectors, 2 * TILE, cols)],
        [SMEM] + [VMEM] * 5,
        [buffer(vectors, 5 * TILE, cols), buffer(4, 5 * TILE, cols)],
        1,
    )(step_counts, k, ax, ay, left, right)
    kept, outer = lax.optimization_barrier((k, edge))
    edge = onward(edge)
    upper = ahead(jnp.concatenate([inner, outer[:, :TILE]], axis=1))
    own, shifted = call(own_kernel, [(pairs, 128), k.shape], [SMEM, VMEM, VMEM], [], 16)(drift, kept, beyond)
    rim_mid = sideways(mid[:, -(DRIFT - TILE) :])
    edge, own, _ = lax.optimization_barrier((edge, own, mid))
    rim_hi = sideways(edge[:, :TILE])
    (gram,) = call(
        gram_kernel, [(world, pairs)], [SMEM] + [VMEM] * 6, [buffer(vectors, DRIFT, cols)], 1
    )(drift, k, shifted, mid, edge, upper, own)
    gram = lax.all_to_all(gram, ("seg", "gx"), 0, 0)
    (product,) = call(last_kernel, [k.shape], [SMEM] + [VMEM] * 6, [], 1)(
        drift, k, mid, edge, rim_mid, rim_hi, upper
    )
    product, gram = lax.optimization_barrier((product, gram))
    cells = world * rows * cols
    gram = jnp.sum(gram, axis=0).reshape(vectors, vectors) / jnp.float32(cells)
    return product[None], gram


def solution(mesh):
    return jax.shard_map(
        body,
        mesh=mesh,
        in_specs=(
            P("seg", None, "gx", None),
            P("seg", "gx", None),
            P("seg", "gx", None),
            P("seg"),
            P("seg"),
        ),
        out_specs=(P("seg", None, "gx", None), P()),
        check_vma=False,
    )
```

```python
import functools
import jax
import jax.numpy as jnp
from jax import lax
from jax.experimental import pallas as pl
from jax.experimental.pallas import tpu as pltpu
from jax.sharding import PartitionSpec as P

STEPS = 4
DRIFT = 16
TILE = 8

ANY = pl.BlockSpec(memory_space=pl.ANY)
VMEM = pl.BlockSpec(memory_space=pltpu.VMEM)
SMEM = pl.BlockSpec(memory_space=pltpu.SMEM)
LIMIT = 12 * 1024 * 1024
FULL = 60 * 1024 * 1024


def shift_pairs(count, by):
    return [(i, (i + by) % count) for i in range(count)]


def weights(ax, ay):
    col = lax.broadcasted_iota(jnp.int32, ax.shape, 1)
    last = ax.shape[1] - 1
    return (
        0.2 - ax,
        0.2 + ax,
        jnp.where(col == last, 0.0, 0.2 - ay),
        jnp.where(col == 0, 0.0, 0.2 + ay),
    )


def step(q, we, ww, wn, ws):
    rows, cols = q.shape
    return (
        0.2 * q
        + we * pltpu.roll(q, rows - 1, 0)
        + ww * pltpu.roll(q, 1, 0)
        + wn * pltpu.roll(q, cols - 1, 1)
        + ws * pltpu.roll(q, 1, 1)
    )


def pack_kernel(k_any, ax_any, ay_any, head_ref, tail_ref, low_ref, high_ref, sems):
    rows = k_any.shape[1]
    vectors = k_any.shape[0]
    copies = []
    for i, (at, target) in enumerate(((0, low_ref), (rows - TILE, high_ref))):
        copies += [
            pltpu.make_async_copy(k_any.at[:, pl.ds(at, TILE)], target.at[pl.ds(0, vectors)], sems.at[i, 0]),
            pltpu.make_async_copy(ax_any.at[pl.ds(at, TILE)], target.at[vectors], sems.at[i, 1]),
            pltpu.make_async_copy(ay_any.at[pl.ds(at, TILE)], target.at[vectors + 1], sems.at[i, 2]),
        ]
    for copy in copies:
        copy.start()
    for copy in copies:
        copy.wait()
    head_ref[...] = low_ref[:, :STEPS]
    tail_ref[...] = high_ref[:, TILE - STEPS :]


def inner_kernel(count_ref, k_ref, ax_ref, ay_ref, mid_ref, beyond_ref, q_ref, w_ref):
    vectors, rows, _ = k_ref.shape
    for i, w in enumerate(weights(ax_ref[...], ay_ref[...])):
        w_ref[i] = w
    q_ref[...] = k_ref[...]
    beyond_ref[...] = k_ref[:, :DRIFT]

    @pl.loop(0, count_ref[0])
    def _(_):
        for b in range(vectors):
            q_ref[b] = step(q_ref[b], w_ref[0], w_ref[1], w_ref[2], w_ref[3])

    mid_ref[...] = q_ref[:, TILE : rows - TILE]


def outer_kernel(count_ref, k_ref, ax_ref, ay_ref, left_ref, right_ref, out_ref, q_ref, w_ref):
    vectors, rows, _ = k_ref.shape

    def around(strip, at):
        return jnp.concatenate(
            [strip[rows - 2 * TILE :], right_ref[at], left_ref[at], strip[: 2 * TILE]], axis=0
        )

    for i, w in enumerate(weights(around(ax_ref, vectors), around(ay_ref, vectors + 1))):
        w_ref[i] = w
    for b in range(vectors):
        q_ref[b] = around(k_ref.at[b], b)

    @pl.loop(0, count_ref[0])
    def _(_):
        for b in range(vectors):
            q_ref[b] = step(q_ref[b], w_ref[0], w_ref[1], w_ref[2], w_ref[3])

    out_ref[:, :TILE] = q_ref[:, TILE : 2 * TILE]
    out_ref[:, TILE:] = q_ref[:, 3 * TILE : 4 * TILE]


def pair_sums(left, right, blocks, vectors, cols):
    sums = []
    half = vectors // 2
    for first in range(0, vectors, half):
        accs = {}
        for block in range(blocks):
            for lane in range(0, cols, 128):
                rs = [right(c, block, lane) for c in range(vectors)]
                for a in range(first, first + half):
                    value = left(a, block, lane)
                    for c in range(vectors):
                        term = value * rs[c]
                        accs[a, c] = accs[a, c] + term if (a, c) in accs else term
        sums += [jnp.sum(accs[a, c], axis=0, keepdims=True) for a in range(first, first + half) for c in range(vectors)]
    return jnp.concatenate(sums, axis=0)


def tile_of(ref, v, block, lane):
    return ref[v, block * TILE : (block + 1) * TILE, lane : lane + 128]


def own_kernel(drift_ref, k_ref, beyond_ref, table_ref, shifted_ref):
    vectors, rows, cols = k_ref.shape
    tile = functools.partial(tile_of, k_ref)
    table_ref[...] = pair_sums(tile, tile, rows // TILE, vectors, cols)
    total = rows + beyond_ref.shape[1]
    by = lax.rem(total - drift_ref[0], total)
    for b in range(vectors):
        joined = jnp.concatenate([k_ref[b], beyond_ref[b]], axis=0)
        shifted_ref[b] = pltpu.roll(joined, by, 0)[:rows]


def gram_kernel(shifted_ref, mid_ref, edge_ref, own_ref, gram_ref):
    vectors, rows, cols = shifted_ref.shape
    blocks = rows // TILE

    def arrived(c, block, lane):
        if block == 0:
            return tile_of(edge_ref, c, 1, lane)
        if block == blocks - 1:
            return tile_of(edge_ref, c, 0, lane)
        return tile_of(mid_ref, c, block - 1, lane)

    table = own_ref[...] - pair_sums(functools.partial(tile_of, shifted_ref), arrived, blocks, vectors, cols)
    ones = jnp.ones((gram_ref.shape[0], 128), jnp.float32)
    gram_ref[...] = lax.dot_general(
        ones, table, (((1,), (1,)), ((), ())),
        precision=lax.Precision.HIGHEST, preferred_element_type=jnp.float32,
    )


def last_kernel(drift_ref, k_ref, mid_ref, edge_ref, rim_mid_ref, rim_hi_ref, product_ref):
    vectors, rows, _ = k_ref.shape
    total = DRIFT + rows
    by = lax.rem(drift_ref[0] + (total - DRIFT), total)
    for b in range(vectors):
        joined = jnp.concatenate(
            [rim_mid_ref[b], rim_hi_ref[b], edge_ref[b, TILE:], mid_ref[b], edge_ref[b, :TILE]], axis=0
        )
        product_ref[b] = k_ref[b] - pltpu.roll(joined, by, 0)[:rows]


def buffer(*shape):
    return pltpu.VMEM(shape, jnp.float32)


def call(kernel, outs, ins, scratch, cost, limit=LIMIT):
    return pl.pallas_call(
        kernel,
        out_shape=[jax.ShapeDtypeStruct(o, jnp.float32) for o in outs],
        in_specs=ins,
        out_specs=[VMEM] * len(outs),
        scratch_shapes=scratch,
        compiler_params=pltpu.CompilerParams(vmem_limit_bytes=limit),
        cost_estimate=pl.CostEstimate(flops=cost << 30, bytes_accessed=4 << 20, transcendentals=0),
    )


def body(krylov, advect_x, advect_y, step_counts, drifts):
    k, ax, ay = krylov[0], advect_x[0], advect_y[0]
    vectors, rows, cols = k.shape
    segs, strips = lax.axis_size("seg"), lax.axis_size("gx")
    world, pairs = segs * strips, vectors * vectors
    half = segs // 2
    onward = functools.partial(lax.ppermute, axis_name="seg", perm=shift_pairs(segs, 1))
    sideways = functools.partial(lax.ppermute, axis_name="gx", perm=shift_pairs(strips, 1))
    backward = functools.partial(lax.ppermute, axis_name="gx", perm=shift_pairs(strips, -1))

    fields = vectors + 2
    head, tail = call(
        pack_kernel,
        [(fields, STEPS, cols)] * 2,
        [ANY] * 3,
        [buffer(fields, TILE, cols), buffer(fields, TILE, cols), pltpu.SemaphoreType.DMA((2, 3))],
        1,
        limit=FULL,
    )(k, ax, ay)
    right = backward(head)
    left = sideways(tail)
    drift = onward(drifts)
    mid, beyond = call(
        inner_kernel,
        [(vectors, rows - 2 * TILE, cols), (vectors, DRIFT, cols)],
        [SMEM, VMEM, VMEM, VMEM],
        [buffer(vectors, rows, cols), buffer(4, rows, cols)],
        64,
    )(step_counts, k, ax, ay)
    beyond, right = lax.optimization_barrier((beyond, right))
    beyond = backward(beyond)
    mid = lax.ppermute(mid, "seg", [(s, s // half * half + (s + 1) % half) for s in range(segs)])
    (edge,) = call(
        outer_kernel,
        [(vectors, 2 * TILE, cols)],
        [SMEM] + [VMEM] * 5,
        [buffer(vectors, 5 * TILE, cols), buffer(4, 5 * TILE, cols)],
        1,
    )(step_counts, k, ax, ay, left, right)
    sent, kept = lax.optimization_barrier((edge, k))
    edge = onward(edge)
    own, shifted = call(own_kernel, [(pairs, 128), k.shape], [SMEM, VMEM, VMEM], [], 16)(drift, kept, beyond)
    held, _ = lax.optimization_barrier((mid, sent))
    crossed = lax.ppermute(held, "seg", [(0, half), (half, 0)])
    mid = jnp.where(lax.axis_index("seg") % half == 0, crossed, mid)
    rim_mid = sideways(mid[:, -(DRIFT - TILE) :])
    edge, own, _ = lax.optimization_barrier((edge, own, mid))
    rim_hi = sideways(edge[:, :TILE])
    (gram,) = call(gram_kernel, [(world, pairs)], [VMEM] * 4, [], 1)(shifted, mid, edge, own)
    gram = lax.all_to_all(gram, ("seg", "gx"), 0, 0)
    (product,) = call(last_kernel, [k.shape], [SMEM] + [VMEM] * 5, [], 1)(
        drift, k, mid, edge, rim_mid, rim_hi
    )
    product, gram = lax.optimization_barrier((product, gram))
    cells = world * rows * cols
    gram = jnp.sum(gram, axis=0).reshape(vectors, vectors) / jnp.float32(cells)
    return product[None], gram


def solution(mesh):
    return jax.shard_map(
        body,
        mesh=mesh,
        in_specs=(
            P("seg", None, "gx", None),
            P("seg", "gx", None),
            P("seg", "gx", None),
            P("seg"),
            P("seg"),
        ),
        out_specs=(P("seg", None, "gx", None), P()),
        check_vma=False,
    )
```
